32 devices in a mesh: groups: 2 (over y), dp: 4 (over z), expert: 2 (over x), mp: 2 (over core).
Axes of the slice: x: 2, y: 2, z: 4, core: 2. Of those that a mesh axis runs over, the one named last changes fastest.
Arguments:
- activations: bfloat16 [96, 6144], P(('groups', 'dp', 'expert')), parts along dimension 0, may hold values from -16 to 16
- gradients: bfloat16 [96, 8192], P(('groups', 'dp', 'expert'), 'mp'), parts along dimension 0, may hold values from -16 to 16
- expert_ids: int32 [96, 1], P(('groups', 'dp', 'expert')), parts along dimension 0, may hold values from 0 to 1; in each aligned block of 6 rows (0 to 5, 6 to 11, ...) at most 5 rows name the same one
- example_ids: int32 [96], P(('groups', 'dp', 'expert')), parts along dimension 0, may hold values from 0 to 31
- example_slots: int32 [64], P('groups'), parts along dimension 0, may hold values from 0 to 31, each once
- eigenbasis: bfloat16 [2, 6144, 6144], P('expert', None, ('dp', 'mp')), may hold values from -0.078125 to 0.078125
- input_eigen: float32 [2, 6144], P('expert', ('dp', 'mp')), may hold values from 0.05 to 5
- output_eigen: float32 [2, 8192], P('expert', 'mp'), may hold values from 0.05 to 5
Outputs:
- influence: float32 [64, 32], P(('groups', 'dp', 'expert')), parts along dimension 0
The draws below stay inside these ranges and needn't reach their ends.
There are 2 independent parts, one for each index of `groups`. The reference program is written for one: setup_inputs(seed, part) draws one part's arguments, and reference() takes and returns one part's arrays. A program takes and returns all parts, laid end to end along the dimension named above; an argument that names none is the same for every part. Nothing has to cross between parts.
Inputs may be any that keep to these rules, and one draw needn't show every extreme that they name: `expert_ids`: within the rows of one source device (aligned blocks of 6 rows) no expert is named by more than 5 rows, and in every draw some expert is named by exactly 5 rows of some block.
All inputs are finite; a program needn't handle non-finite values.
Results may differ from the reference program's by a relative error of at most 0.0003.
Values may be sent and summed in bfloat16 or wider, within the bound.
A program may use at most 128 MiB of HBM per device.

```python
import math
import jax
import jax.numpy as jnp
import numpy as np
from jax import lax

D = 6144
FF = 8192
EPG = 4
EXPERTS = 2
TOK = 6
CAP = 5
ROWS = 48
EXPERT_ROWS = 40
GROUPS = 8
EX = 32
N_DP = 4
N_EXPERT = 2


shared_dims = 4


def shared_part(key, row_count, feature_count, strength):
    coefficient_key, direction_key = jax.random.split(key)
    coefficient = jax.random.normal(coefficient_key, (row_count, 1, shared_dims), jnp.float32)
    direction = jax.random.normal(direction_key, (feature_count // shared_dims, shared_dims), jnp.float32) * strength
    return (coefficient * direction[None]).reshape(row_count, feature_count)


def draw_activations(key, part):
    key = jax.random.fold_in(key, 17)
    noise_key, shared_key = jax.random.split(key, 2)
    noise_part = jax.random.normal(noise_key, (ROWS, D), jnp.float32)
    values = noise_part + shared_part(shared_key, ROWS, D, 1.7)
    return jnp.clip(values, -16.0, 16.0).astype(jnp.bfloat16)


def draw_gradients(key, part):
    key = jax.random.fold_in(key, 23)
    noise_key, shared_key = jax.random.split(key, 2)
    noise_part = jax.random.normal(noise_key, (ROWS, FF), jnp.float32)
    values = noise_part + shared_part(shared_key, ROWS, FF, 1.7)
    return jnp.clip(values, -16.0, 16.0).astype(jnp.bfloat16)


def touch_ends(array, own_key, low, largest):
    place = [jax.random.randint(jax.random.fold_in(own_key, axis), (), 0, length) for axis, length in enumerate(array.shape)]
    widest = array.shape.index(max(array.shape))
    neighbour = place[:widest] + [(place[widest] + 1) % array.shape[widest]] + place[widest + 1:]
    return array.at[tuple(place)].set(low).at[tuple(neighbour)].set(largest)


def levels(stream_key, extent, cuts, smallest, top_value):
    loudness, own = 1.0, jax.random.fold_in(stream_key, 6)
    for dim, parts in cuts:
        draws = jnp.exp(jax.random.uniform(jax.random.fold_in(own, dim), (parts,), jnp.float32, smallest / len(cuts), top_value / len(cuts)))
        loudness = loudness * jnp.repeat(draws, extent[dim] // parts).reshape([-1 if axis == dim else 1 for axis in range(len(extent))])
    return loudness


def assign_block(own_key, own, number, rows, number_of, top, bound, skew):
    sequence = jax.random.permutation(own_key, number_of)
    packed, usual = portions_of(number_of, rows * top, bound, skew, True), portions_of(number_of, rows * top, bound, skew, False)
    places = jnp.arange(number_of)

    def named(lengths, turn):
        used = int((lengths > 0).sum())
        fixed = max(1, used // 4)
        shifted = fixed + (places - fixed + turn * (used - fixed)) % max(1, number_of - fixed)
        return jnp.zeros((number_of,), jnp.int32).at[sequence[jnp.where(places < fixed, places, shifted)]].set(jnp.asarray(lengths, jnp.int32))

    lengths = jnp.where(number % 4 == 0, named(packed, number // 4), named(usual, number - number // 4 - 1))
    mixed = jax.random.permutation(jax.random.fold_in(own, 3), number_of)
    giver, receiver = mixed[0:number_of // 2 * 2:2], mixed[1:number_of // 2 * 2:2]
    margin = jnp.minimum(lengths[giver] - 1, bound - lengths[receiver]) // 2
    margin = jnp.where((giver == sequence[0]) | (receiver == sequence[0]) | (lengths[receiver] == 0), 0, jnp.maximum(margin, 0))
    shifted = jax.random.randint(jax.random.fold_in(own, 4), (number_of // 2,), 0, 1 << 20) % (margin + 1)
    lengths = lengths.at[giver].add(-shifted).at[receiver].add(shifted)
    items = jnp.searchsorted(jnp.cumsum(lengths), jnp.arange(rows * top), side="right").astype(jnp.int32)
    grid = items.reshape(top, rows).T
    grid = grid[jax.random.permutation(jax.random.fold_in(own, 1), rows)]
    turn = jax.random.randint(jax.random.fold_in(own, 2), (rows, 1), 0, top)
    return jnp.take_along_axis(grid, (jnp.arange(top)[None, :] + turn) % top, axis=1)


def portions_of(number_of, total, reach, slope, full):
    portions = [(1 << 20) // math.isqrt(grade ** slope) + 1 for grade in range(1, number_of + 1)]
    largest = reach if full else min(reach, max(-(-total // number_of), total * portions[0] // sum(portions)))
    least = 1 if total - largest >= number_of - 1 else 0
    given, rest = [largest] + [least] * (number_of - 1), total - largest - least * (number_of - 1)
    while rest > 0:
        free = [i for i in range(1, number_of) if given[i] < largest] or [i for i in range(1, number_of) if given[i] < reach]
        pool, left = sum([portions[i] for i in free]), rest
        for i in free:
            more = min(reach - given[i], max(1, left * portions[i] // pool), rest)
            given[i] = given[i] + more
            rest = rest - more
    return np.array(given)


def bell_draw(rng, shape, deviation, limit, cuts=(), kind=jnp.bfloat16):
    array = jax.random.normal(rng, shape, jnp.float32) * deviation
    if len(cuts) > 0:
        array = levels(rng, shape, cuts, -0.22, 0.18) * array
    return jnp.clip(array, min=-limit, max=limit).astype(kind)


def setup_inputs(seed: int = 0, part: int = 0) -> dict:
    seeds = jax.random.split(jax.random.key(seed), 9)
    part_splits = jax.random.split(jax.random.fold_in(seeds[8], part), 9)
    activations = draw_activations(jax.random.fold_in(jax.random.fold_in(seeds[8], part), 71), part)
    gradients = draw_gradients(jax.random.fold_in(jax.random.fold_in(seeds[8], part), 71), part)
    expert_ids_keys = jax.random.split(jax.random.fold_in(part_splits[2], 1), ROWS // TOK)
    expert_ids_turns = jax.random.permutation(jax.random.fold_in(part_splits[2], 3), ROWS // TOK)
    expert_ids = jax.vmap(lambda own, number: assign_block(jax.random.fold_in(part_splits[2], 2), own, number, TOK, EXPERTS, 1, CAP, 2))(expert_ids_keys, expert_ids_turns).reshape((ROWS, 1))
    example_ids = touch_ends(jax.random.randint(part_splits[3], (ROWS,), 0, EX), jax.random.fold_in(part_splits[3], 1), 0, EX - 1).astype(jnp.int32)
    example_slots = jax.random.permutation(part_splits[4], EX).astype(jnp.int32)
    eigenbasis = bell_draw(seeds[5], (EXPERTS, D, D), D ** -0.5, 0.078125, ((0, 2), (2, 8)))
    input_eigen = jnp.clip(jnp.exp(math.log(5.0) - 4.6051702 * jax.random.uniform(seeds[6], (EXPERTS, D), jnp.float32) ** levels(seeds[6], (EXPERTS, D), ((0, 2), (1, 8)), -0.2, 0.2)), 0.05, 5.0)
    output_eigen = jnp.clip(jnp.exp(math.log(5.0) - 4.6051702 * jax.random.uniform(seeds[7], (EXPERTS, FF), jnp.float32) ** levels(seeds[7], (EXPERTS, FF), ((0, 2), (1, 2)), -0.2, 0.2)), 0.05, 5.0)
    return {"activations": activations, "gradients": gradients, "expert_ids": expert_ids, "example_ids": example_ids, "example_slots": example_slots, "eigenbasis": eigenbasis, "input_eigen": input_eigen, "output_eigen": output_eigen}


eigen_floor = 0.01
ridge_term = 500.0

def member_table(slot_list, example_count):
    return (slot_list[:, None] == jnp.arange(example_count, dtype=jnp.int32)[None, :]).astype(jnp.float32)

def solve_system(system_rows, first_row):
    order = system_rows.shape[0]
    square = lax.dynamic_slice_in_dim(system_rows, first_row, order, 1)
    square = square + ridge_term * jnp.eye(order, dtype=system_rows.dtype)
    factor = jnp.linalg.cholesky(square)
    middle = lax.linalg.triangular_solve(factor, system_rows, left_side=True, lower=True)
    return lax.linalg.triangular_solve(factor, middle, left_side=True, lower=True, transpose_a=True)

def reference(activations, gradients, expert_ids, example_ids, example_slots, eigenbasis, input_eigen, output_eigen):
    source_count = N_DP * N_EXPERT
    chosen = expert_ids[:, 0].reshape(source_count, TOK)
    onehot = (chosen[:, :, None] == jnp.arange(EXPERTS, dtype=jnp.int32)[None, None, :]).astype(jnp.int32)
    position = lax.optimization_barrier(jnp.sum((jnp.cumsum(onehot, axis=1) - onehot) * onehot, axis=2))
    sources = jnp.arange(source_count, dtype=jnp.int32)[:, None]
    target = ((chosen * source_count + sources) * CAP + position).reshape(-1).astype(jnp.int32)
    slot_total = EXPERTS * EXPERT_ROWS
    row_slot = jnp.take(example_slots, example_ids).astype(jnp.int32)
    sent_inputs = jnp.zeros((slot_total, D), activations.dtype).at[target].set(activations)
    sent_grads = jnp.zeros((slot_total, FF), gradients.dtype).at[target].set(gradients)
    sent_slots = jnp.full((slot_total,), -1, jnp.int32).at[target].set(row_slot)
    sent_inputs = sent_inputs.reshape(EXPERTS, EXPERT_ROWS, D)
    sent_grads = sent_grads.reshape(EXPERTS, EXPERT_ROWS, FF)
    sent_slots = sent_slots.reshape(EXPERTS, EXPERT_ROWS)

    def per_expert(running, inputs):
        expert_inputs, expert_grads, expert_slots, basis_one, eigen_in, eigen_out = inputs
        rotated = (jnp.dot(expert_inputs.astype(jnp.float32), basis_one.astype(jnp.float32), preferred_element_type=jnp.float32) * lax.rsqrt(eigen_in + eigen_floor)).astype(jnp.bfloat16)
        scaled = (expert_grads.astype(jnp.float32) * lax.rsqrt(eigen_out + eigen_floor)).astype(jnp.bfloat16)
        gram_in = lax.dot_general(rotated.astype(jnp.float32), rotated.astype(jnp.float32), (((1,), (1,)), ((), ())), preferred_element_type=jnp.float32) / D
        gram_out = lax.dot_general(scaled.astype(jnp.float32), scaled.astype(jnp.float32), (((1,), (1,)), ((), ())), preferred_element_type=jnp.float32) / FF
        members = member_table(expert_slots, EX)
        weighted = jnp.dot(gram_in * gram_out, members, precision=lax.Precision.HIGHEST)
        update = lax.dot_general(members, weighted, (((0,), (0,)), ((), ())), precision=lax.Precision.HIGHEST)
        return (running + update, None)
    kernel, _ = lax.scan(per_expert, jnp.zeros((EX, EX), jnp.float32), (sent_inputs, sent_grads, sent_slots, eigenbasis, input_eigen, output_eigen))
    grouped = kernel.reshape(GROUPS, EPG, EX)
    firsts = jnp.arange(GROUPS, dtype=jnp.int32) * EPG
    return jax.vmap(solve_system)(grouped, firsts).reshape(EX, EX)
```

```python
import functools

import jax
import jax.numpy as jnp
from jax import lax
from jax.experimental import pallas as pl
from jax.experimental.pallas import tpu as pltpu
from jax.sharding import PartitionSpec as P

D = 6144
FF = 8192
CAP = 5


eigen_floor = 0.01
ridge_term = 500.0


def shifted(x, axis, by):
    size = lax.axis_size(axis)
    return lax.ppermute(x, axis, [(i, (i + by) % size) for i in range(size)])


def member_table(slot_list, example_count):
    return (slot_list[:, None] == jnp.arange(example_count, dtype=jnp.int32)[None, :]).astype(
        jnp.float32
    )


def solve_system(system_rows, first_row):
    order = system_rows.shape[0]
    square = lax.dynamic_slice_in_dim(system_rows, first_row, order, 1)
    square = square + ridge_term * jnp.eye(order, dtype=system_rows.dtype)
    factor = jnp.linalg.cholesky(square)
    middle = lax.linalg.triangular_solve(factor, system_rows, left_side=True, lower=True)
    return lax.linalg.triangular_solve(factor, middle, left_side=True, lower=True, transpose_a=True)


def on_device(
    activations,
    gradients,
    expert_ids,
    example_ids,
    example_slots,
    eigenbasis,
    input_eigen,
    output_eigen,
):
    data_ways = lax.axis_size("dp")
    expert_ways = lax.axis_size("expert")
    example_count = example_slots.shape[0]
    slot_width = expert_ways * CAP
    chosen = expert_ids[:, 0]
    onehot = (chosen[:, None] == jnp.arange(expert_ways, dtype=jnp.int32)[None, :]).astype(
        jnp.int32
    )
    position = jnp.sum((jnp.cumsum(onehot, axis=0) - onehot) * onehot, axis=1)
    target = chosen * CAP + position
    placing = target[None, :] == jnp.arange(slot_width, dtype=jnp.int32)[:, None]
    placing_table = placing.astype(jnp.bfloat16)
    lookup = (example_ids[:, None] == jnp.arange(example_count, dtype=jnp.int32)[None, :]).astype(
        jnp.int32
    )
    row_slot = jnp.sum(lookup * example_slots[None, :], axis=1)
    send_inputs = jnp.dot(placing_table, activations, preferred_element_type=jnp.float32).astype(
        jnp.bfloat16
    )
    send_grads = jnp.dot(placing_table, gradients, preferred_element_type=jnp.float32).astype(
        jnp.bfloat16
    )
    send_slots = jnp.sum(jnp.where(placing, row_slot[None, :] + 1, 0), axis=1) - 1
    got_inputs, got_grads, got_slots = (
        lax.all_to_all(
            send_inputs.reshape(expert_ways, CAP, -1),
            "expert",
            split_axis=0,
            concat_axis=0,
            tiled=True,
        ),
        lax.all_to_all(
            send_grads.reshape(expert_ways, CAP, -1),
            "expert",
            split_axis=0,
            concat_axis=0,
            tiled=True,
        ),
        lax.all_to_all(
            send_slots.reshape(expert_ways, CAP), "expert", split_axis=0, concat_axis=0, tiled=True
        ),
    )
    own_inputs = got_inputs.reshape(slot_width, -1)
    own_grads = got_grads.reshape(slot_width, -1)
    own_slots = got_slots.reshape(slot_width)
    basis_block = eigenbasis[0]
    scale_in = lax.rsqrt(input_eigen[0] + eigen_floor)
    rotated = (
        jnp.dot(
            lax.all_gather(own_inputs, "dp", axis=0, tiled=True),
            basis_block,
            preferred_element_type=jnp.float32,
        )
        * scale_in
    ).astype(jnp.bfloat16)
    gram_part = (
        lax.dot_general(
            rotated, rotated, (((1,), (1,)), ((), ())), preferred_element_type=jnp.float32
        )
        / D
    )
    dp_index = lax.axis_index("dp")
    gram_in = lax.psum(gram_part, ("dp", "mp"))
    own_gram = lax.dynamic_slice_in_dim(gram_in, dp_index * slot_width, slot_width, 0)
    scaled = (own_grads.astype(jnp.float32) * lax.rsqrt(output_eigen[0] + eigen_floor)).astype(
        jnp.bfloat16
    )
    own_members = member_table(own_slots, example_count)

    def pair_terms(peer_grads, peer_slots, first_row):
        gram_out = (
            lax.dot_general(
                scaled, peer_grads, (((1,), (1,)), ((), ())), preferred_element_type=jnp.float32
            )
            / FF
        )
        weights = lax.dynamic_slice_in_dim(own_gram, first_row, peer_grads.shape[0], 1) * gram_out
        return jnp.dot(
            weights, member_table(peer_slots, example_count), precision=lax.Precision.HIGHEST
        )

    one_way = pair_terms(scaled, own_slots, dp_index * slot_width)
    both_ways = jnp.zeros_like(one_way)
    for offset in range(1, data_ways // 2 + 1):
        peer_grads, peer_slots = shifted((scaled, own_slots), "dp", offset)
        source_index = (dp_index - offset) % data_ways
        contribution = pair_terms(peer_grads, peer_slots, source_index * slot_width)
        if 2 * offset < data_ways:
            both_ways = both_ways + contribution
        else:
            one_way = one_way + contribution
    kernel = lax.dot_general(
        own_members, one_way + both_ways, (((0,), (0,)), ((), ())), precision=lax.Precision.HIGHEST
    )
    mirrored = lax.dot_general(
        own_members, both_ways, (((0,), (0,)), ((), ())), precision=lax.Precision.HIGHEST
    )
    kernel = kernel + mirrored.T
    shares = lax.psum_scatter(kernel, ("dp", "expert", "mp"), scatter_dimension=0, tiled=True)
    system_rows = lax.all_gather(shares, "mp", axis=0, tiled=True)
    first_row = (dp_index * expert_ways + lax.axis_index("expert")) * system_rows.shape[0]
    return solve_system(system_rows, first_row)


MESH = pl.DeviceIdType.MESH
PAD = 8
LANES = 128
HALF_CHUNKS = 2


def fused_kernel(
    sizes,
    act_hbm,
    grad_hbm,
    expert_ids,
    example_ids,
    example_slots,
    basis_hbm,
    in_eigen_hbm,
    out_eigen_hbm,
    out_ref,
    act_v,
    grad_v,
    in_eigen,
    out_eigen,
    basis,
    gathered,
    grad_send,
    grad_got,
    part_send,
    part_got,
    kernel_send,
    kernel_got,
    local_sem,
    basis_sem,
    send_sem,
    half_sem,
    other_sem,
    grad_sem,
    part_sem,
    kernel_sem,
):
    data_ways, expert_ways, tok, example_count = sizes
    blocks = data_ways * expert_ways
    order = example_count // blocks
    rows = blocks * PAD
    z, x, m = lax.axis_index("dp"), lax.axis_index("expert"), lax.axis_index("mp")
    own = z * expert_ways + x
    chunk = gathered.shape[3]
    quarter = out_eigen.shape[1]
    chunks = gathered.shape[0]

    def at(zz, xx, mm):
        return {"dp": zz, "expert": xx, "mp": mm}

    def turn(i, by, size):
        return lax.rem(i + by, size)

    z_turns = sorted(range(1, data_ways), key=lambda d: (min(d, data_ways - d), d))
    x_turns = range(1, expert_ways)
    other = 1 - m

    barrier = pltpu.get_barrier_semaphore()
    peers = 0
    for dz in range(data_ways):
        for dx in range(expert_ways):
            for dm in range(2):
                if dz or dx or dm:
                    pl.semaphore_signal(
                        barrier,
                        inc=1,
                        device_id=at(
                            turn(z, dz, data_ways), turn(x, dx, expert_ways), turn(m, dm, 2)
                        ),
                        device_id_type=MESH,
                    )
                    peers += 1

    act_copy = pltpu.make_async_copy(act_hbm, act_v, local_sem.at[0])
    act_copy.start()
    grad_copy = pltpu.make_async_copy(grad_hbm, grad_v, local_sem.at[1])
    grad_copy.start()
    chunk_order = [
        m * HALF_CHUNKS + i for i in range(HALF_CHUNKS)
    ] + [other * HALF_CHUNKS + i for i in range(HALF_CHUNKS)]
    basis_copies = []
    for i, c in enumerate(chunk_order):
        span = pl.ds(pl.multiple_of(c * chunk, chunk), chunk)
        copy = pltpu.make_async_copy(
            basis_hbm.at[0, span, :], basis.at[span, :], basis_sem.at[i]
        )
        copy.start()
        basis_copies.append(copy)
    in_copy = pltpu.make_async_copy(in_eigen_hbm, in_eigen, local_sem.at[2])
    in_copy.start()
    out_copy = pltpu.make_async_copy(
        out_eigen_hbm.at[:, pl.ds(pl.multiple_of(z * quarter, quarter), quarter)],
        out_eigen,
        local_sem.at[3],
    )
    out_copy.start()

    def padded(value):
        value = value.astype(jnp.float32)
        fill = jnp.zeros((PAD - tok, value.shape[1]), jnp.float32)
        return jnp.concatenate([value, fill], axis=0).astype(jnp.bfloat16)

    act_copy.wait()
    for c in range(chunks):
        gathered[c, own] = padded(act_v[:, c * chunk : (c + 1) * chunk])

    sends = []

    def send(source, target, sem, device):
        copy = pltpu.make_async_remote_copy(
            src_ref=source,
            dst_ref=target,
            send_sem=send_sem.at[len(sends)],
            recv_sem=sem,
            device_id=device,
            device_id_type=MESH,
        )
        copy.start()
        sends.append(copy)

    def arrived(target, sem):
        pltpu.make_async_copy(target, target, sem).wait()

    pl.semaphore_wait(barrier, peers)

    for i in range(HALF_CHUNKS):
        block = gathered.at[m * HALF_CHUNKS + i, own]
        for dx in x_turns:
            send(block, block, half_sem.at[i, own], at(z, turn(x, dx, expert_ways), m))
        for dz in reversed(z_turns):
            send(block, block, half_sem.at[i, own], at(turn(z, dz, data_ways), x, m))

    row_at = lax.broadcasted_iota(jnp.int32, (PAD, LANES), 0)
    lane_at = lax.broadcasted_iota(jnp.int32, (PAD, LANES), 1)
    table = jnp.zeros((PAD, LANES), jnp.float32)
    for r in range(tok):
        place = example_slots[example_ids[r]]
        expert = expert_ids[r, 0]
        spread = LANES // 2 + place // order * PAD + place % order
        hit = (
            (lane_at == place) | (lane_at == example_count + expert) | (lane_at == spread)
        ) & (row_at == r)
        table = jnp.where(hit, 1.0, table)
    table = table.astype(jnp.bfloat16)
    grad_copy.wait()
    for q in range(data_ways):
        grad_send[q, :, :quarter] = padded(grad_v[:, q * quarter : (q + 1) * quarter])
        grad_send[q, :, quarter:] = table
    grad_got[own] = grad_send[z]
    for dz in [0] + z_turns:
        for dx in range(expert_ways):
            if dz or dx:
                zz = turn(z, dz, data_ways)
                send(
                    grad_send.at[zz],
                    grad_got.at[own],
                    grad_sem.at[own],
                    at(zz, turn(x, dx, expert_ways), m),
                )

    for i in range(HALF_CHUNKS):
        c = m * HALF_CHUNKS + i
        for dz in z_turns:
            b = turn(z, dz, data_ways) * expert_ways + x
            block = gathered.at[c, b]
            arrived(block, half_sem.at[i, b])
            for dx in x_turns:
                send(block, block, half_sem.at[i, b], at(z, turn(x, dx, expert_ways), m))
            send(block, block, other_sem.at[i, b], at(z, x, other))
        for dz in [0] + z_turns:
            for dx in x_turns:
                b = turn(z, dz, data_ways) * expert_ways + turn(x, dx, expert_ways)
                block = gathered.at[c, b]
                arrived(block, half_sem.at[i, b])
                send(block, block, other_sem.at[i, b], at(z, x, other))

    total = jnp.zeros((rows, basis.shape[1]), jnp.float32)
    for i, c in enumerate(chunk_order):
        if i >= HALF_CHUNKS:
            for dz in range(data_ways):
                for dx in range(expert_ways):
                    if dz or dx:
                        b = turn(z, dz, data_ways) * expert_ways + turn(x, dx, expert_ways)
                        arrived(gathered.at[c, b], other_sem.at[i - HALF_CHUNKS, b])
        basis_copies[i].wait()
        left = jnp.concatenate(
            [gathered[c, b].astype(jnp.float32) for b in range(blocks)], axis=0
        ).astype(jnp.bfloat16)
        span = pl.ds(pl.multiple_of(c * chunk, chunk), chunk)
        total = total + jnp.dot(left, basis[span, :], preferred_element_type=jnp.float32)

    def gram(value):
        return lax.dot_general(
            value, value, (((1,), (1,)), ((), ())), preferred_element_type=jnp.float32
        )

    in_copy.wait()
    rotated = (total * lax.rsqrt(in_eigen[...] + eigen_floor)).astype(jnp.bfloat16)
    gram_in = gram(rotated) / D

    for dz in range(data_ways):
        for dx in range(expert_ways):
            if dz or dx:
                b = turn(z, dz, data_ways) * expert_ways + turn(x, dx, expert_ways)
                arrived(grad_got.at[b], grad_sem.at[b])
    out_copy.wait()
    grads = jnp.concatenate(
        [grad_got[b, :, :quarter].astype(jnp.float32) for b in range(blocks)], axis=0
    )
    scaled = (grads * lax.rsqrt(out_eigen[...] + eigen_floor)).astype(jnp.bfloat16)
    gram_out = gram(scaled) / FF

    part_send[...] = jnp.concatenate([gram_in, gram_out], axis=1).reshape(blocks, PAD, LANES)
    mine = z * 2 + m
    for dz in [0] + z_turns:
        for dm in range(2):
            if dz or dm:
                zz, mm = turn(z, dz, data_ways), turn(m, dm, 2)
                send(
                    part_send.at[zz * 2 + mm],
                    part_got.at[mine],
                    part_sem.at[mine],
                    at(zz, x, mm),
                )
    tables = jnp.concatenate(
        [grad_got[b, :, quarter:].astype(jnp.float32) for b in range(blocks)], axis=0
    )

    def members(value):
        lanes = lax.broadcasted_iota(jnp.int32, value.shape, 1)
        chosen = jnp.where(lanes == example_count + x, value, 0.0)
        return value * jnp.sum(chosen, axis=1, keepdims=True)

    every_member = members(tables)
    own_member = members(grad_got[mine, :, quarter:].astype(jnp.float32))
    sums = part_send[mine]
    for dz in range(data_ways):
        for dm in range(2):
            if dz or dm:
                b = turn(z, dz, data_ways) * 2 + turn(m, dm, 2)
                arrived(part_got.at[b], part_sem.at[b])
                sums = sums + part_got[b]
    weights = sums[:, :rows] * sums[:, rows:]
    right = jnp.dot(
        weights,
        every_member,
        precision=lax.Precision.HIGHEST,
        preferred_element_type=jnp.float32,
    )
    pairs = lax.dot_general(
        own_member,
        right,
        (((0,), (0,)), ((), ())),
        precision=lax.Precision.HIGHEST,
        preferred_element_type=jnp.float32,
    )
    kernel_send[...] = pairs[LANES // 2 :].reshape(blocks, PAD, LANES)
    place = own * 2 + m
    for dz in [0] + z_turns:
        for dx in range(expert_ways):
            for dm in range(2):
                if dz or dx or dm:
                    zz, xx, mm = turn(z, dz, data_ways), turn(x, dx, expert_ways), turn(m, dm, 2)
                    send(
                        kernel_send.at[zz * expert_ways + xx],
                        kernel_got.at[place],
                        kernel_sem.at[place],
                        at(zz, xx, mm),
                    )
    kernel_got[place] = kernel_send[own]
    for dz in range(data_ways):
        for dx in range(expert_ways):
            for dm in range(2):
                if dz or dx or dm:
                    zz, xx, mm = turn(z, dz, data_ways), turn(x, dx, expert_ways), turn(m, dm, 2)
                    b = (zz * expert_ways + xx) * 2 + mm
                    arrived(kernel_got.at[b], kernel_sem.at[b])
    system = kernel_got[0]
    for b in range(1, blocks * 2):
        system = system + kernel_got[b]

    work = system
    for k in range(order):
        column = jnp.sum(jnp.where(lane_at == own * order + k, system, 0.0), axis=1, keepdims=True)
        column = column + jnp.where(row_at == k, ridge_term, 0.0)
        work = jnp.where(lane_at == LANES // 2 + k, column, work)
    for k in range(order):
        column = jnp.sum(jnp.where(lane_at == LANES // 2 + k, work, 0.0), axis=1, keepdims=True)
        pivot_row = work[k : k + 1, :] / column[k : k + 1, :]
        work = jnp.where(row_at == k, pivot_row, work - column * pivot_row)
    out_ref[...] = work[:order, :example_count]
    for copy in sends:
        copy.wait_send()


def fused(
    activations,
    gradients,
    expert_ids,
    example_ids,
    example_slots,
    eigenbasis,
    input_eigen,
    output_eigen,
):
    data_ways = lax.axis_size("dp")
    expert_ways = lax.axis_size("expert")
    tok = activations.shape[0]
    example_count = example_slots.shape[0]
    blocks = data_ways * expert_ways
    depth, width = eigenbasis.shape[1:]
    chunks = 2 * HALF_CHUNKS
    chunk = depth // chunks
    quarter = gradients.shape[1] // data_ways
    z_sends, x_sends = data_ways - 1, expert_ways - 1
    send_count = (
        HALF_CHUNKS * (z_sends + x_sends + z_sends * (x_sends + 1) + data_ways * x_sends)
        + (blocks - 1)
        + (data_ways * 2 - 1)
        + (blocks * 2 - 1)
    )
    dma = pltpu.SemaphoreType.DMA
    anywhere = pl.BlockSpec(memory_space=pl.ANY)
    scalars = pl.BlockSpec(memory_space=pltpu.SMEM)
    return pl.pallas_call(
        functools.partial(fused_kernel, (data_ways, expert_ways, tok, example_count)),
        out_shape=jax.ShapeDtypeStruct((example_count // blocks, example_count), jnp.float32),
        in_specs=[anywhere, anywhere, scalars, scalars, scalars, anywhere, anywhere, anywhere],
        out_specs=pl.BlockSpec(memory_space=pltpu.VMEM),
        scratch_shapes=[
            pltpu.VMEM(activations.shape, jnp.bfloat16),
            pltpu.VMEM(gradients.shape, jnp.bfloat16),
            pltpu.VMEM(input_eigen.shape, jnp.float32),
            pltpu.VMEM((1, quarter), jnp.float32),
            pltpu.VMEM((depth, width), jnp.bfloat16),
            pltpu.VMEM((chunks, blocks, PAD, chunk), jnp.bfloat16),
            pltpu.VMEM((data_ways, PAD, quarter + LANES), jnp.bfloat16),
            pltpu.VMEM((blocks, PAD, quarter + LANES), jnp.bfloat16),
            pltpu.VMEM((blocks, PAD, LANES), jnp.float32),
            pltpu.VMEM((blocks, PAD, LANES), jnp.float32),
            pltpu.VMEM((blocks, PAD, LANES), jnp.float32),
            pltpu.VMEM((blocks * 2, PAD, LANES), jnp.float32),
            dma((4,)),
            dma((chunks,)),
            dma((send_count,)),
            dma((HALF_CHUNKS, blocks)),
            dma((HALF_CHUNKS, blocks)),
            dma((blocks,)),
            dma((blocks,)),
            dma((blocks * 2,)),
        ],
        compiler_params=pltpu.CompilerParams(
            collective_id=0, has_side_effects=True, vmem_limit_bytes=48 * 1024 * 1024
        ),
    )(
        activations,
        gradients,
        expert_ids,
        example_ids,
        example_slots,
        eigenbasis,
        input_eigen,
        output_eigen,
    )


def fits_fused(mesh, tok, example_count):
    data_ways, expert_ways = mesh.shape["dp"], mesh.shape["expert"]
    blocks = data_ways * expert_ways
    order = example_count // blocks
    return (
        mesh.shape["mp"] == 2
        and data_ways * 2 == blocks
        and blocks * PAD * 2 == LANES
        and tok <= PAD
        and order <= PAD
        and example_count + expert_ways <= LANES // 2
    )


def on_any_slice(mesh, activations, gradients, expert_ids, example_ids, example_slots, *factors):
    use = fits_fused(mesh, activations.shape[0], example_slots.shape[0])
    return (fused if use else on_device)(
        activations, gradients, expert_ids, example_ids, example_slots, *factors
    )


def solution(mesh):
    placed = (
        P(("groups", "dp", "expert"), None),
        P(("groups", "dp", "expert"), "mp"),
        P(("groups", "dp", "expert"), None),
        P(("groups", "dp", "expert")),
        P("groups"),
        P("expert", None, ("dp", "mp")),
        P("expert", ("dp", "mp")),
        P("expert", "mp"),
    )
    return jax.shard_map(
        functools.partial(on_any_slice, mesh),
        mesh=mesh,
        in_specs=placed,
        out_specs=P(("groups", "dp", "expert"), None),
        check_vma=False,
    )
```

```python
import functools

import jax
import jax.numpy as jnp
from jax import lax
from jax.experimental import pallas as pl
from jax.experimental.pallas import tpu as pltpu
from jax.sharding import PartitionSpec as P

D = 6144
FF = 8192
CAP = 5


eigen_floor = 0.01
ridge_term = 500.0


def shifted(x, axis, by):
    size = lax.axis_size(axis)
    return lax.ppermute(x, axis, [(i, (i + by) % size) for i in range(size)])


def member_table(slot_list, example_count):
    return (slot_list[:, None] == jnp.arange(example_count, dtype=jnp.int32)[None, :]).astype(
        jnp.float32
    )


def solve_system(system_rows, first_row):
    order = system_rows.shape[0]
    square = lax.dynamic_slice_in_dim(system_rows, first_row, order, 1)
    square = square + ridge_term * jnp.eye(order, dtype=system_rows.dtype)
    factor = jnp.linalg.cholesky(square)
    middle = lax.linalg.triangular_solve(factor, system_rows, left_side=True, lower=True)
    return lax.linalg.triangular_solve(factor, middle, left_side=True, lower=True, transpose_a=True)


def on_device(
    activations,
    gradients,
    expert_ids,
    example_ids,
    example_slots,
    eigenbasis,
    input_eigen,
    output_eigen,
):
    data_ways = lax.axis_size("dp")
    expert_ways = lax.axis_size("expert")
    example_count = example_slots.shape[0]
    slot_width = expert_ways * CAP
    chosen = expert_ids[:, 0]
    onehot = (chosen[:, None] == jnp.arange(expert_ways, dtype=jnp.int32)[None, :]).astype(
        jnp.int32
    )
    position = jnp.sum((jnp.cumsum(onehot, axis=0) - onehot) * onehot, axis=1)
    target = chosen * CAP + position
    placing = target[None, :] == jnp.arange(slot_width, dtype=jnp.int32)[:, None]
    placing_table = placing.astype(jnp.bfloat16)
    lookup = (example_ids[:, None] == jnp.arange(example_count, dtype=jnp.int32)[None, :]).astype(
        jnp.int32
    )
    row_slot = jnp.sum(lookup * example_slots[None, :], axis=1)
    send_inputs = jnp.dot(placing_table, activations, preferred_element_type=jnp.float32).astype(
        jnp.bfloat16
    )
    send_grads = jnp.dot(placing_table, gradients, preferred_element_type=jnp.float32).astype(
        jnp.bfloat16
    )
    send_slots = jnp.sum(jnp.where(placing, row_slot[None, :] + 1, 0), axis=1) - 1
    got_inputs, got_grads, got_slots = (
        lax.all_to_all(
            send_inputs.reshape(expert_ways, CAP, -1),
            "expert",
            split_axis=0,
            concat_axis=0,
            tiled=True,
        ),
        lax.all_to_all(
            send_grads.reshape(expert_ways, CAP, -1),
            "expert",
            split_axis=0,
            concat_axis=0,
            tiled=True,
        ),
        lax.all_to_all(
            send_slots.reshape(expert_ways, CAP), "expert", split_axis=0, concat_axis=0, tiled=True
        ),
    )
    own_inputs = got_inputs.reshape(slot_width, -1)
    own_grads = got_grads.reshape(slot_width, -1)
    own_slots = got_slots.reshape(slot_width)
    basis_block = eigenbasis[0]
    scale_in = lax.rsqrt(input_eigen[0] + eigen_floor)
    rotated = (
        jnp.dot(
            lax.all_gather(own_inputs, "dp", axis=0, tiled=True),
            basis_block,
            preferred_element_type=jnp.float32,
        )
        * scale_in
    ).astype(jnp.bfloat16)
    gram_part = (
        lax.dot_general(
            rotated, rotated, (((1,), (1,)), ((), ())), preferred_element_type=jnp.float32
        )
        / D
    )
    dp_index = lax.axis_index("dp")
    gram_in = lax.psum(gram_part, ("dp", "mp"))
    own_gram = lax.dynamic_slice_in_dim(gram_in, dp_index * slot_width, slot_width, 0)
    scaled = (own_grads.astype(jnp.float32) * lax.rsqrt(output_eigen[0] + eigen_floor)).astype(
        jnp.bfloat16
    )
    own_members = member_table(own_slots, example_count)

    def pair_terms(peer_grads, peer_slots, first_row):
        gram_out = (
            lax.dot_general(
                scaled, peer_grads, (((1,), (1,)), ((), ())), preferred_element_type=jnp.float32
            )
            / FF
        )
        weights = lax.dynamic_slice_in_dim(own_gram, first_row, peer_grads.shape[0], 1) * gram_out
        return jnp.dot(
            weights, member_table(peer_slots, example_count), precision=lax.Precision.HIGHEST
        )

    one_way = pair_terms(scaled, own_slots, dp_index * slot_width)
    both_ways = jnp.zeros_like(one_way)
    for offset in range(1, data_ways // 2 + 1):
        peer_grads, peer_slots = shifted((scaled, own_slots), "dp", offset)
        source_index = (dp_index - offset) % data_ways
        contribution = pair_terms(peer_grads, peer_slots, source_index * slot_width)
        if 2 * offset < data_ways:
            both_ways = both_ways + contribution
        else:
            one_way = one_way + contribution
    kernel = lax.dot_general(
        own_members, one_way + both_ways, (((0,), (0,)), ((), ())), precision=lax.Precision.HIGHEST
    )
    mirrored = lax.dot_general(
        own_members, both_ways, (((0,), (0,)), ((), ())), precision=lax.Precision.HIGHEST
    )
    kernel = kernel + mirrored.T
    shares = lax.psum_scatter(kernel, ("dp", "expert", "mp"), scatter_dimension=0, tiled=True)
    system_rows = lax.all_gather(shares, "mp", axis=0, tiled=True)
    first_row = (dp_index * expert_ways + lax.axis_index("expert")) * system_rows.shape[0]
    return solve_system(system_rows, first_row)


MESH = pl.DeviceIdType.MESH
PAD = 8
LANES = 128
HALF_CHUNKS = 1
ACT_GROUPS = 2 * HALF_CHUNKS
GRAD, PART, KERNEL = ACT_GROUPS, ACT_GROUPS + 1, ACT_GROUPS + 2


def fused_kernel(
    sizes,
    act_hbm,
    grad_hbm,
    expert_ids_hbm,
    example_ids_hbm,
    example_slots_hbm,
    basis_hbm,
    in_eigen_hbm,
    out_eigen_hbm,
    out_ref,
    expert_ids,
    example_ids,
    example_slots,
    act_v,
    grad_v,
    in_eigen,
    out_eigen,
    basis,
    gathered,
    grad_send,
    grad_got,
    part_send,
    part_got,
    kernel_send,
    kernel_got,
    local_sem,
    basis_sem,
    send_sem,
    half_sem,
    other_sem,
    grad_sem,
    part_sem,
    kernel_sem,
):
    data_ways, expert_ways, tok, example_count = sizes
    blocks = data_ways * expert_ways
    order = example_count // blocks
    rows = blocks * PAD
    z, x, m = lax.axis_index("dp"), lax.axis_index("expert"), lax.axis_index("mp")
    own = z * expert_ways + x
    chunk = gathered.shape[3]
    quarter = out_eigen.shape[1]
    chunks = gathered.shape[0]

    def at(zz, xx, mm):
        return {"dp": zz, "expert": xx, "mp": mm}

    def turn(i, by, size):
        return lax.rem(i + by, size)

    z_turns = sorted(range(1, data_ways), key=lambda d: (min(d, data_ways - d), d))
    x_turns = range(1, expert_ways)
    other = 1 - m

    barrier = pltpu.get_barrier_semaphore()
    peers = 0
    for dz in range(data_ways):
        for dx in range(expert_ways):
            for dm in range(2):
                if dz or dx or dm:
                    pl.semaphore_signal(
                        barrier,
                        inc=1,
                        device_id=at(
                            turn(z, dz, data_ways), turn(x, dx, expert_ways), turn(m, dm, 2)
                        ),
                        device_id_type=MESH,
                    )
                    peers += 1

    act_copy = pltpu.make_async_copy(act_hbm, act_v, local_sem.at[0])
    act_copy.start()
    id_copies = [
        pltpu.make_async_copy(source, target, local_sem.at[4 + i])
        for i, (source, target) in enumerate(
            (
                (expert_ids_hbm, expert_ids),
                (example_ids_hbm, example_ids),
                (example_slots_hbm, example_slots),
            )
        )
    ]
    for copy in id_copies:
        copy.start()
    grad_copy = pltpu.make_async_copy(grad_hbm, grad_v, local_sem.at[1])
    grad_copy.start()
    chunk_order = [
        m * HALF_CHUNKS + i for i in range(HALF_CHUNKS)
    ] + [other * HALF_CHUNKS + i for i in range(HALF_CHUNKS)]
    basis_copies = []
    for i, c in enumerate(chunk_order):
        span = pl.ds(pl.multiple_of(c * chunk, chunk), chunk)
        copy = pltpu.make_async_copy(
            basis_hbm.at[0, span, :], basis.at[span, :], basis_sem.at[i]
        )
        copy.start()
        basis_copies.append(copy)
    in_copy = pltpu.make_async_copy(in_eigen_hbm, in_eigen, local_sem.at[2])
    in_copy.start()
    out_copy = pltpu.make_async_copy(
        out_eigen_hbm.at[:, pl.ds(pl.multiple_of(z * quarter, quarter), quarter)],
        out_eigen,
        local_sem.at[3],
    )
    out_copy.start()

    def padded(value):
        value = value.astype(jnp.float32)
        fill = jnp.zeros((PAD - tok, value.shape[1]), jnp.float32)
        return jnp.concatenate([value, fill], axis=0).astype(jnp.bfloat16)

    act_copy.wait()
    for c in range(chunks):
        gathered[c, own] = padded(act_v[:, c * chunk : (c + 1) * chunk])

    act_sends = []

    def send(source, target, sem, device, group=None):
        if group is None:
            group = len(act_sends) // (blocks - 1)
            act_sends.append(group)
        pltpu.make_async_remote_copy(
            src_ref=source,
            dst_ref=target,
            send_sem=send_sem.at[group],
            recv_sem=sem,
            device_id=device,
            device_id_type=MESH,
        ).start()

    def arrived(target, sem):
        pltpu.make_async_copy(target, target, sem).wait()

    pl.semaphore_wait(barrier, peers)

    for i in range(HALF_CHUNKS):
        block = gathered.at[m * HALF_CHUNKS + i, own]
        for dx in x_turns:
            send(block, block, half_sem.at[i, own], at(z, turn(x, dx, expert_ways), m))
        for dz in reversed(z_turns):
            send(block, block, half_sem.at[i, own], at(turn(z, dz, data_ways), x, m))

    row_at = lax.broadcasted_iota(jnp.int32, (PAD, LANES), 0)
    lane_at = lax.broadcasted_iota(jnp.int32, (PAD, LANES), 1)
    table = jnp.zeros((PAD, LANES), jnp.float32)
    for copy in id_copies:
        copy.wait()
    for r in range(tok):
        place = example_slots[example_ids[r]]
        expert = expert_ids[0, r]
        spread = LANES // 2 + place // order * PAD + place % order
        hit = (
            (lane_at == place) | (lane_at == example_count + expert) | (lane_at == spread)
        ) & (row_at == r)
        table = jnp.where(hit, 1.0, table)
    table = table.astype(jnp.bfloat16)
    grad_copy.wait()
    for q in range(data_ways):
        grad_send[q, :, :quarter] = padded(grad_v[:, q * quarter : (q + 1) * quarter])
        grad_send[q, :, quarter:] = table
    grad_got[own] = grad_send[z]
    for dz in [0] + z_turns:
        for dx in range(expert_ways):
            if dz or dx:
                zz = turn(z, dz, data_ways)
                send(
                    grad_send.at[zz],
                    grad_got.at[own],
                    grad_sem.at[0],
                    at(zz, turn(x, dx, expert_ways), m),
                    group=GRAD,
                )

    for i in range(HALF_CHUNKS):
        c = m * HALF_CHUNKS + i
        for dz in z_turns:
            b = turn(z, dz, data_ways) * expert_ways + x
            block = gathered.at[c, b]
            arrived(block, half_sem.at[i, b])
            for dx in x_turns:
                send(block, block, half_sem.at[i, b], at(z, turn(x, dx, expert_ways), m))
            send(block, block, other_sem.at[i], at(z, x, other))
        for dz in [0] + z_turns:
            for dx in x_turns:
                b = turn(z, dz, data_ways) * expert_ways + turn(x, dx, expert_ways)
                block = gathered.at[c, b]
                arrived(block, half_sem.at[i, b])
                send(block, block, other_sem.at[i], at(z, x, other))

    total = jnp.zeros((rows, basis.shape[1]), jnp.float32)
    for i, c in enumerate(chunk_order):
        if i >= HALF_CHUNKS:
            arrived(gathered.at[c, pl.ds(0, blocks - 1)], other_sem.at[i - HALF_CHUNKS])
        basis_copies[i].wait()
        left = jnp.concatenate(
            [gathered[c, b].astype(jnp.float32) for b in range(blocks)], axis=0
        ).astype(jnp.bfloat16)
        span = pl.ds(pl.multiple_of(c * chunk, chunk), chunk)
        total = total + jnp.dot(left, basis[span, :], preferred_element_type=jnp.float32)

    def gram(value):
        return lax.dot_general(
            value, value, (((1,), (1,)), ((), ())), preferred_element_type=jnp.float32
        )

    in_copy.wait()
    rotated = (total * lax.rsqrt(in_eigen[...] + eigen_floor)).astype(jnp.bfloat16)
    gram_in = gram(rotated) / D

    arrived(grad_got.at[pl.ds(0, blocks - 1)], grad_sem.at[0])
    out_copy.wait()
    grads = jnp.concatenate(
        [grad_got[b, :, :quarter].astype(jnp.float32) for b in range(blocks)], axis=0
    )
    scaled = (grads * lax.rsqrt(out_eigen[...] + eigen_floor)).astype(jnp.bfloat16)
    gram_out = gram(scaled) / FF

    part_send[...] = jnp.concatenate([gram_in, gram_out], axis=1).reshape(blocks, PAD, LANES)
    mine = z * 2 + m
    for dz in [0] + z_turns:
        for dm in range(2):
            if dz or dm:
                zz, mm = turn(z, dz, data_ways), turn(m, dm, 2)
                send(
                    part_send.at[zz * 2 + mm],
                    part_got.at[mine],
                    part_sem.at[0],
                    at(zz, x, mm),
                    group=PART,
                )
    tables = jnp.concatenate(
        [grad_got[b, :, quarter:].astype(jnp.float32) for b in range(blocks)], axis=0
    )

    def members(value):
        lanes = lax.broadcasted_iota(jnp.int32, value.shape, 1)
        chosen = jnp.where(lanes == example_count + x, value, 0.0)
        return value * jnp.sum(chosen, axis=1, keepdims=True)

    every_member = members(tables)
    own_member = members(grad_got[mine, :, quarter:].astype(jnp.float32))
    part_got[mine] = part_send[mine]
    arrived(part_got.at[pl.ds(0, blocks - 1)], part_sem.at[0])
    sums = jnp.sum(part_got[...], axis=0)
    weights = sums[:, :rows] * sums[:, rows:]
    right = jnp.dot(
        weights,
        every_member,
        precision=lax.Precision.HIGHEST,
        preferred_element_type=jnp.float32,
    )
    pairs = lax.dot_general(
        own_member,
        right,
        (((0,), (0,)), ((), ())),
        precision=lax.Precision.HIGHEST,
        preferred_element_type=jnp.float32,
    )
    kernel_send[...] = pairs[LANES // 2 :].reshape(blocks, PAD, LANES)
    place = own * 2 + m
    for dz in [0] + z_turns:
        for dx in range(expert_ways):
            for dm in range(2):
                if dz or dx or dm:
                    zz, xx, mm = turn(z, dz, data_ways), turn(x, dx, expert_ways), turn(m, dm, 2)
                    send(
                        kernel_send.at[zz * expert_ways + xx],
                        kernel_got.at[place],
                        kernel_sem.at[0],
                        at(zz, xx, mm),
                        group=KERNEL,
                    )
    kernel_got[place] = kernel_send[own]
    arrived(kernel_got.at[pl.ds(0, blocks * 2 - 1)], kernel_sem.at[0])
    system = jnp.sum(kernel_got[...], axis=0)

    work = system
    for k in range(order):
        column = jnp.sum(jnp.where(lane_at == own * order + k, system, 0.0), axis=1, keepdims=True)
        column = column + jnp.where(row_at == k, ridge_term, 0.0)
        work = jnp.where(lane_at == LANES // 2 + k, column, work)
    for k in range(order):
        column = jnp.sum(jnp.where(lane_at == LANES // 2 + k, work, 0.0), axis=1, keepdims=True)
        pivot_row = work[k : k + 1, :] / column[k : k + 1, :]
        work = jnp.where(row_at == k, pivot_row, work - column * pivot_row)
    out_ref[...] = work[:order, :example_count]
    for group in range(ACT_GROUPS):
        arrived(gathered.at[0, pl.ds(0, blocks - 1)], send_sem.at[group])
    arrived(grad_got.at[pl.ds(0, blocks - 1)], send_sem.at[GRAD])
    arrived(part_got.at[pl.ds(0, blocks - 1)], send_sem.at[PART])
    arrived(kernel_got.at[pl.ds(0, blocks * 2 - 1)], send_sem.at[KERNEL])


def fused(
    activations,
    gradients,
    expert_ids,
    example_ids,
    example_slots,
    eigenbasis,
    input_eigen,
    output_eigen,
):
    data_ways = lax.axis_size("dp")
    expert_ways = lax.axis_size("expert")
    tok = activations.shape[0]
    example_count = example_slots.shape[0]
    blocks = data_ways * expert_ways
    depth, width = eigenbasis.shape[1:]
    chunks = 2 * HALF_CHUNKS
    chunk = depth // chunks
    quarter = gradients.shape[1] // data_ways
    dma = pltpu.SemaphoreType.DMA
    far = pl.BlockSpec(memory_space=pltpu.HBM)
    return pl.pallas_call(
        functools.partial(fused_kernel, (data_ways, expert_ways, tok, example_count)),
        out_shape=jax.ShapeDtypeStruct((example_count // blocks, example_count), jnp.float32),
        in_specs=[far] * 8,
        out_specs=pl.BlockSpec(memory_space=pltpu.VMEM),
        scratch_shapes=[
            pltpu.SMEM((1, tok), jnp.int32),
            pltpu.SMEM((tok,), jnp.int32),
            pltpu.SMEM((example_count,), jnp.int32),
            pltpu.VMEM(activations.shape, jnp.bfloat16),
            pltpu.VMEM(gradients.shape, jnp.bfloat16),
            pltpu.VMEM(input_eigen.shape, jnp.float32),
            pltpu.VMEM((1, quarter), jnp.float32),
            pltpu.VMEM((depth, width), jnp.bfloat16),
            pltpu.VMEM((chunks, blocks, PAD, chunk), jnp.bfloat16),
            pltpu.VMEM((data_ways, PAD, quarter + LANES), jnp.bfloat16),
            pltpu.VMEM((blocks, PAD, quarter + LANES), jnp.bfloat16),
            pltpu.VMEM((blocks, PAD, LANES), jnp.float32),
            pltpu.VMEM((blocks, PAD, LANES), jnp.float32),
            pltpu.VMEM((blocks, PAD, LANES), jnp.float32),
            pltpu.VMEM((blocks * 2, PAD, LANES), jnp.float32),
            dma((7,)),
            dma((chunks,)),
            dma((KERNEL + 1,)),
            dma((HALF_CHUNKS, blocks)),
            dma((HALF_CHUNKS,)),
            dma((1,)),
            dma((1,)),
            dma((1,)),
        ],
        compiler_params=pltpu.CompilerParams(
            collective_id=0, has_side_effects=True, vmem_limit_bytes=60 * 1024 * 1024
        ),
    )(
        activations,
        gradients,
        expert_ids.T,
        example_ids,
        example_slots,
        eigenbasis,
        input_eigen,
        output_eigen,
    )


def fits_fused(mesh, tok, example_count):
    data_ways, expert_ways = mesh.shape["dp"], mesh.shape["expert"]
    blocks = data_ways * expert_ways
    order = example_count // blocks
    return (
        mesh.shape["mp"] == 2
        and data_ways * 2 == blocks
        and blocks * PAD * 2 == LANES
        and tok <= PAD
        and order <= PAD
        and example_count + expert_ways <= LANES // 2
    )


def on_any_slice(mesh, activations, gradients, expert_ids, example_ids, example_slots, *factors):
    use = fits_fused(mesh, activations.shape[0], example_slots.shape[0])
    return (fused if use else on_device)(
        activations, gradients, expert_ids, example_ids, example_slots, *factors
    )


def solution(mesh):
    placed = (
        P(("groups", "dp", "expert"), None),
        P(("groups", "dp", "expert"), "mp"),
        P(("groups", "dp", "expert"), None),
        P(("groups", "dp", "expert")),
        P("groups"),
        P("expert", None, ("dp", "mp")),
        P("expert", ("dp", "mp")),
        P("expert", "mp"),
    )
    return jax.shard_map(
        functools.partial(on_any_slice, mesh),
        mesh=mesh,
        in_specs=placed,
        out_specs=P(("groups", "dp", "expert"), None),
        check_vma=False,
    )
```

```python
import functools

import jax
import jax.numpy as jnp
from jax import lax
from jax.experimental import pallas as pl
from jax.experimental.pallas import tpu as pltpu
from jax.sharding import PartitionSpec as P

D = 6144
FF = 8192
CAP = 5


eigen_floor = 0.01
ridge_term = 500.0


def shifted(x, axis, by):
    size = lax.axis_size(axis)
    return lax.ppermute(x, axis, [(i, (i + by) % size) for i in range(size)])


def member_table(slot_list, example_count):
    return (slot_list[:, None] == jnp.arange(example_count, dtype=jnp.int32)[None, :]).astype(
        jnp.float32
    )


def solve_system(system_rows, first_row):
    order = system_rows.shape[0]
    square = lax.dynamic_slice_in_dim(system_rows, first_row, order, 1)
    square = square + ridge_term * jnp.eye(order, dtype=system_rows.dtype)
    factor = jnp.linalg.cholesky(square)
    middle = lax.linalg.triangular_solve(factor, system_rows, left_side=True, lower=True)
    return lax.linalg.triangular_solve(factor, middle, left_side=True, lower=True, transpose_a=True)


def on_device(
    activations,
    gradients,
    expert_ids,
    example_ids,
    example_slots,
    eigenbasis,
    input_eigen,
    output_eigen,
):
    data_ways = lax.axis_size("dp")
    expert_ways = lax.axis_size("expert")
    example_count = example_slots.shape[0]
    slot_width = expert_ways * CAP
    chosen = expert_ids[:, 0]
    onehot = (chosen[:, None] == jnp.arange(expert_ways, dtype=jnp.int32)[None, :]).astype(
        jnp.int32
    )
    position = jnp.sum((jnp.cumsum(onehot, axis=0) - onehot) * onehot, axis=1)
    target = chosen * CAP + position
    placing = target[None, :] == jnp.arange(slot_width, dtype=jnp.int32)[:, None]
    placing_table = placing.astype(jnp.bfloat16)
    lookup = (example_ids[:, None] == jnp.arange(example_count, dtype=jnp.int32)[None, :]).astype(
        jnp.int32
    )
    row_slot = jnp.sum(lookup * example_slots[None, :], axis=1)
    send_inputs = jnp.dot(placing_table, activations, preferred_element_type=jnp.float32).astype(
        jnp.bfloat16
    )
    send_grads = jnp.dot(placing_table, gradients, preferred_element_type=jnp.float32).astype(
        jnp.bfloat16
    )
    send_slots = jnp.sum(jnp.where(placing, row_slot[None, :] + 1, 0), axis=1) - 1
    got_inputs, got_grads, got_slots = (
        lax.all_to_all(
            send_inputs.reshape(expert_ways, CAP, -1),
            "expert",
            split_axis=0,
            concat_axis=0,
            tiled=True,
        ),
        lax.all_to_all(
            send_grads.reshape(expert_ways, CAP, -1),
            "expert",
            split_axis=0,
            concat_axis=0,
            tiled=True,
        ),
        lax.all_to_all(
            send_slots.reshape(expert_ways, CAP), "expert", split_axis=0, concat_axis=0, tiled=True
        ),
    )
    own_inputs = got_inputs.reshape(slot_width, -1)
    own_grads = got_grads.reshape(slot_width, -1)
    own_slots = got_slots.reshape(slot_width)
    basis_block = eigenbasis[0]
    scale_in = lax.rsqrt(input_eigen[0] + eigen_floor)
    rotated = (
        jnp.dot(
            lax.all_gather(own_inputs, "dp", axis=0, tiled=True),
            basis_block,
            preferred_element_type=jnp.float32,
        )
        * scale_in
    ).astype(jnp.bfloat16)
    gram_part = (
        lax.dot_general(
            rotated, rotated, (((1,), (1,)), ((), ())), preferred_element_type=jnp.float32
        )
        / D
    )
    dp_index = lax.axis_index("dp")
    gram_in = lax.psum(gram_part, ("dp", "mp"))
    own_gram = lax.dynamic_slice_in_dim(gram_in, dp_index * slot_width, slot_width, 0)
    scaled = (own_grads.astype(jnp.float32) * lax.rsqrt(output_eigen[0] + eigen_floor)).astype(
        jnp.bfloat16
    )
    own_members = member_table(own_slots, example_count)

    def pair_terms(peer_grads, peer_slots, first_row):
        gram_out = (
            lax.dot_general(
                scaled, peer_grads, (((1,), (1,)), ((), ())), preferred_element_type=jnp.float32
            )
            / FF
        )
        weights = lax.dynamic_slice_in_dim(own_gram, first_row, peer_grads.shape[0], 1) * gram_out
        return jnp.dot(
            weights, member_table(peer_slots, example_count), precision=lax.Precision.HIGHEST
        )

    one_way = pair_terms(scaled, own_slots, dp_index * slot_width)
    both_ways = jnp.zeros_like(one_way)
    for offset in range(1, data_ways // 2 + 1):
        peer_grads, peer_slots = shifted((scaled, own_slots), "dp", offset)
        source_index = (dp_index - offset) % data_ways
        contribution = pair_terms(peer_grads, peer_slots, source_index * slot_width)
        if 2 * offset < data_ways:
            both_ways = both_ways + contribution
        else:
            one_way = one_way + contribution
    kernel = lax.dot_general(
        own_members, one_way + both_ways, (((0,), (0,)), ((), ())), precision=lax.Precision.HIGHEST
    )
    mirrored = lax.dot_general(
        own_members, both_ways, (((0,), (0,)), ((), ())), precision=lax.Precision.HIGHEST
    )
    kernel = kernel + mirrored.T
    shares = lax.psum_scatter(kernel, ("dp", "expert", "mp"), scatter_dimension=0, tiled=True)
    system_rows = lax.all_gather(shares, "mp", axis=0, tiled=True)
    first_row = (dp_index * expert_ways + lax.axis_index("expert")) * system_rows.shape[0]
    return solve_system(system_rows, first_row)


MESH = pl.DeviceIdType.MESH
PAD = 8
LANES = 128
HALF_CHUNKS = 1
ACT_GROUPS = 2 * HALF_CHUNKS
GRAD, PART, KERNEL = ACT_GROUPS, ACT_GROUPS + 1, ACT_GROUPS + 2


def fused_kernel(
    sizes,
    act_hbm,
    grad_hbm,
    expert_ids_hbm,
    example_ids_hbm,
    example_slots_hbm,
    basis_hbm,
    in_eigen_hbm,
    out_eigen_hbm,
    out_ref,
    expert_ids,
    example_ids,
    example_slots,
    act_v,
    grad_v,
    in_eigen,
    out_eigen,
    basis,
    gathered,
    grad_send,
    grad_got,
    part_send,
    part_got,
    kernel_send,
    kernel_got,
    total,
    local_sem,
    basis_sem,
    send_sem,
    half_sem,
    other_sem,
    grad_sem,
    part_sem,
    kernel_sem,
):
    data_ways, expert_ways, tok, example_count = sizes
    blocks = data_ways * expert_ways
    order = example_count // blocks
    rows = blocks * PAD
    z, x, m = lax.axis_index("dp"), lax.axis_index("expert"), lax.axis_index("mp")
    own = z * expert_ways + x
    chunk = gathered.shape[3]
    quarter = out_eigen.shape[1]
    chunks = gathered.shape[0]

    def at(zz, xx, mm):
        return {"dp": zz, "expert": xx, "mp": mm}

    def turn(i, by, size):
        return lax.rem(i + by, size)

    z_turns = sorted(range(1, data_ways), key=lambda d: (min(d, data_ways - d), d))
    x_turns = range(1, expert_ways)
    other = 1 - m

    barrier = pltpu.get_barrier_semaphore()
    peers = 0
    for dz in range(data_ways):
        for dx in range(expert_ways):
            for dm in range(2):
                if (dz or dx or dm) and not (dx and dm):
                    pl.semaphore_signal(
                        barrier,
                        inc=1,
                        device_id=at(
                            turn(z, dz, data_ways), turn(x, dx, expert_ways), turn(m, dm, 2)
                        ),
                        device_id_type=MESH,
                    )
                    peers += 1

    act_copy = pltpu.make_async_copy(act_hbm, act_v, local_sem.at[0])
    act_copy.start()
    id_copies = [
        pltpu.make_async_copy(source, target, local_sem.at[4 + i])
        for i, (source, target) in enumerate(
            (
                (expert_ids_hbm, expert_ids),
                (example_ids_hbm, example_ids),
                (example_slots_hbm, example_slots),
            )
        )
    ]
    for copy in id_copies:
        copy.start()
    grad_copy = pltpu.make_async_copy(grad_hbm, grad_v, local_sem.at[1])
    grad_copy.start()
    chunk_order = [
        m * HALF_CHUNKS + i for i in range(HALF_CHUNKS)
    ] + [other * HALF_CHUNKS + i for i in range(HALF_CHUNKS)]
    basis_copies = []
    for i, c in enumerate(chunk_order):
        span = pl.ds(pl.multiple_of(c * chunk, chunk), chunk)
        copy = pltpu.make_async_copy(
            basis_hbm.at[0, span, :], basis.at[span, :], basis_sem.at[i]
        )
        copy.start()
        basis_copies.append(copy)
    in_copy = pltpu.make_async_copy(in_eigen_hbm, in_eigen, local_sem.at[2])
    in_copy.start()
    out_copy = pltpu.make_async_copy(
        out_eigen_hbm.at[:, pl.ds(pl.multiple_of(z * quarter, quarter), quarter)],
        out_eigen,
        local_sem.at[3],
    )
    out_copy.start()

    def padded(value):
        value = value.astype(jnp.float32)
        fill = jnp.zeros((PAD - tok, value.shape[1]), jnp.float32)
        return jnp.concatenate([value, fill], axis=0).astype(jnp.bfloat16)

    act_copy.wait()
    for c in range(chunks):
        gathered[c, own] = padded(act_v[:, c * chunk : (c + 1) * chunk])

    act_sends = []

    def send(source, target, sem, device, group=None):
        if group is None:
            group = len(act_sends) // (blocks - 1)
            act_sends.append(group)
        pltpu.make_async_remote_copy(
            src_ref=source,
            dst_ref=target,
            send_sem=send_sem.at[group],
            recv_sem=sem,
            device_id=device,
            device_id_type=MESH,
        ).start()

    def arrived(target, sem):
        pltpu.make_async_copy(target, target, sem).wait()

    pl.semaphore_wait(barrier, peers)

    for i in range(HALF_CHUNKS):
        block = gathered.at[m * HALF_CHUNKS + i, own]
        for dx in x_turns:
            send(block, block, half_sem.at[i, own], at(z, turn(x, dx, expert_ways), m))
        for dz in reversed(z_turns):
            send(block, block, half_sem.at[i, own], at(turn(z, dz, data_ways), x, m))

    row_at = lax.broadcasted_iota(jnp.int32, (PAD, LANES), 0)
    lane_at = lax.broadcasted_iota(jnp.int32, (PAD, LANES), 1)
    table = jnp.zeros((PAD, LANES), jnp.float32)
    for copy in id_copies:
        copy.wait()
    for r in range(tok):
        place = example_slots[example_ids[r]]
        expert = expert_ids[0, r]
        spread = LANES // 2 + place // order * PAD + place % order
        hit = (
            (lane_at == place) | (lane_at == example_count + expert) | (lane_at == spread)
        ) & (row_at == r)
        table = jnp.where(hit, 1.0, table)
    table = table.astype(jnp.bfloat16)
    grad_copy.wait()
    for q in range(data_ways):
        grad_send[q, :, :quarter] = padded(grad_v[:, q * quarter : (q + 1) * quarter])
        grad_send[q, :, quarter:] = table
    grad_got[own] = grad_send[z]
    for dz in [0] + z_turns:
        for dx in range(expert_ways):
            if dz or dx:
                zz = turn(z, dz, data_ways)
                send(
                    grad_send.at[zz],
                    grad_got.at[own],
                    grad_sem.at[0],
                    at(zz, turn(x, dx, expert_ways), m),
                    group=GRAD,
                )

    for i in range(HALF_CHUNKS):
        c = m * HALF_CHUNKS + i
        for dz in z_turns:
            b = turn(z, dz, data_ways) * expert_ways + x
            block = gathered.at[c, b]
            arrived(block, half_sem.at[i, b])
            for dx in x_turns:
                send(block, block, half_sem.at[i, b], at(z, turn(x, dx, expert_ways), m))
            send(block, block, other_sem.at[i], at(z, x, other))
        for dz in [0] + z_turns:
            for dx in x_turns:
                b = turn(z, dz, data_ways) * expert_ways + turn(x, dx, expert_ways)
                block = gathered.at[c, b]
                arrived(block, half_sem.at[i, b])
                send(block, block, other_sem.at[i], at(z, x, other))

    def add_product(c, first):
        left = jnp.concatenate(
            [gathered[c, b].astype(jnp.float32) for b in range(blocks)], axis=0
        ).astype(jnp.bfloat16)
        span = pl.ds(pl.multiple_of(c * chunk, chunk), chunk)
        product = jnp.dot(left, basis[span, :], preferred_element_type=jnp.float32)
        total[...] = product if first else product + total[...]

    def gram(value):
        return lax.dot_general(
            value, value, (((1,), (1,)), ((), ())), preferred_element_type=jnp.float32
        )

    for i in range(HALF_CHUNKS):
        basis_copies[i].wait()
        add_product(chunk_order[i], i == 0)
    arrived(grad_got.at[pl.ds(0, blocks - 1)], grad_sem.at[0])
    out_copy.wait()
    grads = jnp.concatenate(
        [grad_got[b, :, :quarter].astype(jnp.float32) for b in range(blocks)], axis=0
    )
    scaled = (grads * lax.rsqrt(out_eigen[...] + eigen_floor)).astype(jnp.bfloat16)
    gram_out = gram(scaled) / FF
    mine = z * 2 + m
    tables = jnp.concatenate(
        [grad_got[b, :, quarter:].astype(jnp.float32) for b in range(blocks)], axis=0
    )

    def members(value):
        lanes = lax.broadcasted_iota(jnp.int32, value.shape, 1)
        chosen = jnp.where(lanes == example_count + x, value, 0.0)
        return value * jnp.sum(chosen, axis=1, keepdims=True)

    every_member = members(tables).astype(jnp.bfloat16)
    own_member = members(
        jnp.concatenate(
            [grad_got[z * 2 + i, :, quarter:].astype(jnp.float32) for i in range(2)], axis=0
        )
    )
    own_member = jnp.concatenate([own_member] * 3, axis=0).astype(jnp.bfloat16)

    def terms(value):
        high = value.astype(jnp.bfloat16).astype(jnp.float32)
        middle = (value - high).astype(jnp.bfloat16).astype(jnp.float32)
        return jnp.concatenate([high, middle, value - high - middle], axis=0).astype(jnp.bfloat16)

    for i in range(HALF_CHUNKS):
        c = chunk_order[HALF_CHUNKS + i]
        arrived(gathered.at[c, pl.ds(0, blocks - 1)], other_sem.at[i])
        basis_copies[HALF_CHUNKS + i].wait()
        add_product(c, False)

    in_copy.wait()
    rotated = (total[...] * lax.rsqrt(in_eigen[...] + eigen_floor)).astype(jnp.bfloat16)
    gram_in = gram(rotated) / D

    part_send[...] = jnp.concatenate([gram_in, gram_out], axis=1).reshape(
        data_ways, 2 * PAD, LANES
    )
    for dz in [0] + z_turns:
        for dm in range(2):
            if dz or dm:
                zz, mm = turn(z, dz, data_ways), turn(m, dm, 2)
                send(
                    part_send.at[zz],
                    part_got.at[mine],
                    part_sem.at[0],
                    at(zz, x, mm),
                    group=PART,
                )
    part_got[mine] = part_send[z]
    arrived(part_got.at[pl.ds(0, blocks - 1)], part_sem.at[0])
    sums = jnp.sum(part_got[...], axis=0)
    weights = sums[:, :rows] * sums[:, rows:]
    right = jnp.dot(terms(weights), every_member, preferred_element_type=jnp.float32)
    right = right[: 2 * PAD] + right[2 * PAD : 4 * PAD] + right[4 * PAD :]
    pairs = lax.dot_general(
        own_member,
        terms(right),
        (((0,), (0,)), ((), ())),
        preferred_element_type=jnp.float32,
    )
    kernel_send[...] = pairs[LANES // 2 :].reshape(blocks, PAD, LANES)
    for dz in [0] + z_turns:
        for dx in range(expert_ways):
            if dz or dx:
                zz, xx = turn(z, dz, data_ways), turn(x, dx, expert_ways)
                send(
                    kernel_send.at[zz * expert_ways + xx],
                    kernel_got.at[own],
                    kernel_sem.at[0],
                    at(zz, xx, m),
                    group=KERNEL,
                )
    kernel_got[own] = kernel_send[own]
    arrived(kernel_got.at[pl.ds(0, blocks - 1)], kernel_sem.at[0])
    system = jnp.sum(kernel_got[...], axis=0)

    work = system
    for k in range(order):
        column = jnp.sum(jnp.where(lane_at == own * order + k, system, 0.0), axis=1, keepdims=True)
        column = column + jnp.where(row_at == k, ridge_term, 0.0)
        work = jnp.where(lane_at == LANES // 2 + k, column, work)
    for k in range(order):
        column = jnp.sum(jnp.where(lane_at == LANES // 2 + k, work, 0.0), axis=1, keepdims=True)
        pivot_row = work[k : k + 1, :] / column[k : k + 1, :]
        work = jnp.where(row_at == k, pivot_row, work - column * pivot_row)
    out_ref[...] = work[:order, :example_count]
    for group in range(ACT_GROUPS):
        arrived(gathered.at[0, pl.ds(0, blocks - 1)], send_sem.at[group])
    arrived(grad_got.at[pl.ds(0, blocks - 1)], send_sem.at[GRAD])
    arrived(part_got.at[pl.ds(0, blocks - 1)], send_sem.at[PART])
    arrived(kernel_got.at[pl.ds(0, blocks - 1)], send_sem.at[KERNEL])


def fused(
    activations,
    gradients,
    expert_ids,
    example_ids,
    example_slots,
    eigenbasis,
    input_eigen,
    output_eigen,
):
    data_ways = lax.axis_size("dp")
    expert_ways = lax.axis_size("expert")
    tok = activations.shape[0]
    example_count = example_slots.shape[0]
    blocks = data_ways * expert_ways
    depth, width = eigenbasis.shape[1:]
    chunks = 2 * HALF_CHUNKS
    chunk = depth // chunks
    quarter = gradients.shape[1] // data_ways
    dma = pltpu.SemaphoreType.DMA
    far = pl.BlockSpec(memory_space=pltpu.HBM)
    return pl.pallas_call(
        functools.partial(fused_kernel, (data_ways, expert_ways, tok, example_count)),
        out_shape=jax.ShapeDtypeStruct((example_count // blocks, example_count), jnp.float32),
        in_specs=[far] * 8,
        out_specs=pl.BlockSpec(memory_space=pltpu.VMEM),
        scratch_shapes=[
            pltpu.SMEM((1, tok), jnp.int32),
            pltpu.SMEM((tok,), jnp.int32),
            pltpu.SMEM((example_count,), jnp.int32),
            pltpu.VMEM(activations.shape, jnp.bfloat16),
            pltpu.VMEM(gradients.shape, jnp.bfloat16),
            pltpu.VMEM(input_eigen.shape, jnp.float32),
            pltpu.VMEM((1, quarter), jnp.float32),
            pltpu.VMEM((depth, width), jnp.bfloat16),
            pltpu.VMEM((chunks, blocks, PAD, chunk), jnp.bfloat16),
            pltpu.VMEM((data_ways, PAD, quarter + LANES), jnp.bfloat16),
            pltpu.VMEM((blocks, PAD, quarter + LANES), jnp.bfloat16),
            pltpu.VMEM((data_ways, 2 * PAD, LANES), jnp.float32),
            pltpu.VMEM((blocks, 2 * PAD, LANES), jnp.float32),
            pltpu.VMEM((blocks, PAD, LANES), jnp.float32),
            pltpu.VMEM((blocks, PAD, LANES), jnp.float32),
            pltpu.VMEM((blocks * PAD, width), jnp.float32),
            dma((7,)),
            dma((chunks,)),
            dma((KERNEL + 1,)),
            dma((HALF_CHUNKS, blocks)),
            dma((HALF_CHUNKS,)),
            dma((1,)),
            dma((1,)),
            dma((1,)),
        ],
        compiler_params=pltpu.CompilerParams(
            collective_id=0, has_side_effects=True, vmem_limit_bytes=60 * 1024 * 1024
        ),
    )(
        activations,
        gradients,
        expert_ids.T,
        example_ids,
        example_slots,
        eigenbasis,
        input_eigen,
        output_eigen,
    )


def fits_fused(mesh, tok, example_count):
    data_ways, expert_ways = mesh.shape["dp"], mesh.shape["expert"]
    blocks = data_ways * expert_ways
    order = example_count // blocks
    return (
        mesh.shape["mp"] == 2
        and data_ways * 2 == blocks
        and blocks * PAD * 2 == LANES
        and tok <= PAD
        and order <= PAD
        and example_count + expert_ways <= LANES // 2
    )


def on_any_slice(mesh, activations, gradients, expert_ids, example_ids, example_slots, *factors):
    use = fits_fused(mesh, activations.shape[0], example_slots.shape[0])
    return (fused if use else on_device)(
        activations, gradients, expert_ids, example_ids, example_slots, *factors
    )


def solution(mesh):
    placed = (
        P(("groups", "dp", "expert"), None),
        P(("groups", "dp", "expert"), "mp"),
        P(("groups", "dp", "expert"), None),
        P(("groups", "dp", "expert")),
        P("groups"),
        P("expert", None, ("dp", "mp")),
        P("expert", ("dp", "mp")),
        P("expert", "mp"),
    )
    return jax.shard_map(
        functools.partial(on_any_slice, mesh),
        mesh=mesh,
        in_specs=placed,
        out_specs=P(("groups", "dp", "expert"), None),
        check_vma=False,
    )
```

```python
import functools

import jax
import jax.numpy as jnp
from jax import lax
from jax.experimental import pallas as pl
from jax.experimental.pallas import tpu as pltpu
from jax.sharding import PartitionSpec as P

D = 6144
FF = 8192
CAP = 5


eigen_floor = 0.01
ridge_term = 500.0


def shifted(x, axis, by):
    size = lax.axis_size(axis)
    return lax.ppermute(x, axis, [(i, (i + by) % size) for i in range(size)])


def member_table(slot_list, example_count):
    return (slot_list[:, None] == jnp.arange(example_count, dtype=jnp.int32)[None, :]).astype(
        jnp.float32
    )


def solve_system(system_rows, first_row):
    order = system_rows.shape[0]
    square = lax.dynamic_slice_in_dim(system_rows, first_row, order, 1)
    square = square + ridge_term * jnp.eye(order, dtype=system_rows.dtype)
    factor = jnp.linalg.cholesky(square)
    middle = lax.linalg.triangular_solve(factor, system_rows, left_side=True, lower=True)
    return lax.linalg.triangular_solve(factor, middle, left_side=True, lower=True, transpose_a=True)


def on_device(
    activations,
    gradients,
    expert_ids,
    example_ids,
    example_slots,
    eigenbasis,
    input_eigen,
    output_eigen,
):
    data_ways = lax.axis_size("dp")
    expert_ways = lax.axis_size("expert")
    example_count = example_slots.shape[0]
    slot_width = expert_ways * CAP
    chosen = expert_ids[:, 0]
    onehot = (chosen[:, None] == jnp.arange(expert_ways, dtype=jnp.int32)[None, :]).astype(
        jnp.int32
    )
    position = jnp.sum((jnp.cumsum(onehot, axis=0) - onehot) * onehot, axis=1)
    target = chosen * CAP + position
    placing = target[None, :] == jnp.arange(slot_width, dtype=jnp.int32)[:, None]
    placing_table = placing.astype(jnp.bfloat16)
    lookup = (example_ids[:, None] == jnp.arange(example_count, dtype=jnp.int32)[None, :]).astype(
        jnp.int32
    )
    row_slot = jnp.sum(lookup * example_slots[None, :], axis=1)
    send_inputs = jnp.dot(placing_table, activations, preferred_element_type=jnp.float32).astype(
        jnp.bfloat16
    )
    send_grads = jnp.dot(placing_table, gradients, preferred_element_type=jnp.float32).astype(
        jnp.bfloat16
    )
    send_slots = jnp.sum(jnp.where(placing, row_slot[None, :] + 1, 0), axis=1) - 1
    got_inputs, got_grads, got_slots = (
        lax.all_to_all(
            send_inputs.reshape(expert_ways, CAP, -1),
            "expert",
            split_axis=0,
            concat_axis=0,
            tiled=True,
        ),
        lax.all_to_all(
            send_grads.reshape(expert_ways, CAP, -1),
            "expert",
            split_axis=0,
            concat_axis=0,
            tiled=True,
        ),
        lax.all_to_all(
            send_slots.reshape(expert_ways, CAP), "expert", split_axis=0, concat_axis=0, tiled=True
        ),
    )
    own_inputs = got_inputs.reshape(slot_width, -1)
    own_grads = got_grads.reshape(slot_width, -1)
    own_slots = got_slots.reshape(slot_width)
    basis_block = eigenbasis[0]
    scale_in = lax.rsqrt(input_eigen[0] + eigen_floor)
    rotated = (
        jnp.dot(
            lax.all_gather(own_inputs, "dp", axis=0, tiled=True),
            basis_block,
            preferred_element_type=jnp.float32,
        )
        * scale_in
    ).astype(jnp.bfloat16)
    gram_part = (
        lax.dot_general(
            rotated, rotated, (((1,), (1,)), ((), ())), preferred_element_type=jnp.float32
        )
        / D
    )
    dp_index = lax.axis_index("dp")
    gram_in = lax.psum(gram_part, ("dp", "mp"))
    own_gram = lax.dynamic_slice_in_dim(gram_in, dp_index * slot_width, slot_width, 0)
    scaled = (own_grads.astype(jnp.float32) * lax.rsqrt(output_eigen[0] + eigen_floor)).astype(
        jnp.bfloat16
    )
    own_members = member_table(own_slots, example_count)

    def pair_terms(peer_grads, peer_slots, first_row):
        gram_out = (
            lax.dot_general(
                scaled, peer_grads, (((1,), (1,)), ((), ())), preferred_element_type=jnp.float32
            )
            / FF
        )
        weights = lax.dynamic_slice_in_dim(own_gram, first_row, peer_grads.shape[0], 1) * gram_out
        return jnp.dot(
            weights, member_table(peer_slots, example_count), precision=lax.Precision.HIGHEST
        )

    one_way = pair_terms(scaled, own_slots, dp_index * slot_width)
    both_ways = jnp.zeros_like(one_way)
    for offset in range(1, data_ways // 2 + 1):
        peer_grads, peer_slots = shifted((scaled, own_slots), "dp", offset)
        source_index = (dp_index - offset) % data_ways
        contribution = pair_terms(peer_grads, peer_slots, source_index * slot_width)
        if 2 * offset < data_ways:
            both_ways = both_ways + contribution
        else:
            one_way = one_way + contribution
    kernel = lax.dot_general(
        own_members, one_way + both_ways, (((0,), (0,)), ((), ())), precision=lax.Precision.HIGHEST
    )
    mirrored = lax.dot_general(
        own_members, both_ways, (((0,), (0,)), ((), ())), precision=lax.Precision.HIGHEST
    )
    kernel = kernel + mirrored.T
    shares = lax.psum_scatter(kernel, ("dp", "expert", "mp"), scatter_dimension=0, tiled=True)
    system_rows = lax.all_gather(shares, "mp", axis=0, tiled=True)
    first_row = (dp_index * expert_ways + lax.axis_index("expert")) * system_rows.shape[0]
    return solve_system(system_rows, first_row)


MESH = pl.DeviceIdType.MESH
PAD = 8
LANES = 128
HALF_CHUNKS = 1
ACT_GROUPS = 2 * HALF_CHUNKS
GRAD, PART, KERNEL = ACT_GROUPS, ACT_GROUPS + 1, ACT_GROUPS + 2


def fused_kernel(
    sizes,
    act_hbm,
    grad_hbm,
    expert_ids_hbm,
    example_ids_hbm,
    example_slots_hbm,
    basis_hbm,
    in_eigen_hbm,
    out_eigen_hbm,
    out_ref,
    expert_ids,
    example_ids,
    example_slots,
    act_v,
    grad_v,
    in_eigen,
    out_eigen,
    basis,
    gathered,
    grad_send,
    grad_got,
    part_send,
    part_got,
    kernel_send,
    kernel_got,
    total,
    local_sem,
    basis_sem,
    send_sem,
    half_sem,
    other_sem,
    grad_sem,
    part_sem,
    kernel_sem,
):
    data_ways, expert_ways, tok, example_count = sizes
    blocks = data_ways * expert_ways
    order = example_count // blocks
    rows = blocks * PAD
    z, x, m = lax.axis_index("dp"), lax.axis_index("expert"), lax.axis_index("mp")
    own = z * expert_ways + x
    chunk = gathered.shape[3]
    quarter = out_eigen.shape[1]
    chunks = gathered.shape[0]

    def at(zz, xx, mm):
        return {"dp": zz, "expert": xx, "mp": mm}

    def turn(i, by, size):
        return lax.rem(i + by, size)

    z_turns = sorted(range(1, data_ways), key=lambda d: (min(d, data_ways - d), d))
    x_turns = range(1, expert_ways)
    other = 1 - m

    barrier = pltpu.get_barrier_semaphore()
    peers = 0
    for dz in range(data_ways):
        for dx in range(expert_ways):
            for dm in range(2):
                if (dz or dx or dm) and not (dx and dm):
                    pl.semaphore_signal(
                        barrier,
                        inc=1,
                        device_id=at(
                            turn(z, dz, data_ways), turn(x, dx, expert_ways), turn(m, dm, 2)
                        ),
                        device_id_type=MESH,
                    )
                    peers += 1

    act_copy = pltpu.make_async_copy(act_hbm, act_v, local_sem.at[0])
    act_copy.start()
    id_copies = [
        pltpu.make_async_copy(source, target, local_sem.at[4 + i])
        for i, (source, target) in enumerate(
            (
                (expert_ids_hbm, expert_ids),
                (example_ids_hbm, example_ids),
                (example_slots_hbm, example_slots),
            )
        )
    ]
    for copy in id_copies:
        copy.start()
    grad_copy = pltpu.make_async_copy(grad_hbm, grad_v, local_sem.at[1])
    grad_copy.start()
    chunk_order = [
        m * HALF_CHUNKS + i for i in range(HALF_CHUNKS)
    ] + [other * HALF_CHUNKS + i for i in range(HALF_CHUNKS)]
    basis_copies = []
    for i, c in enumerate(chunk_order):
        span = pl.ds(pl.multiple_of(c * chunk, chunk), chunk)
        copy = pltpu.make_async_copy(
            basis_hbm.at[0, span, :], basis.at[span, :], basis_sem.at[i]
        )
        copy.start()
        basis_copies.append(copy)
    in_copy = pltpu.make_async_copy(in_eigen_hbm, in_eigen, local_sem.at[2])
    in_copy.start()
    out_copy = pltpu.make_async_copy(
        out_eigen_hbm.at[:, pl.ds(pl.multiple_of(z * quarter, quarter), quarter)],
        out_eigen,
        local_sem.at[3],
    )
    out_copy.start()

    def padded(value):
        value = value.astype(jnp.float32)
        fill = jnp.zeros((PAD - tok, value.shape[1]), jnp.float32)
        return jnp.concatenate([value, fill], axis=0).astype(jnp.bfloat16)

    act_copy.wait()
    for c in range(chunks):
        gathered[c, own] = padded(act_v[:, c * chunk : (c + 1) * chunk])

    act_sends = []

    def send(source, target, sem, device, group=None):
        if group is None:
            group = len(act_sends) // (blocks - 1)
            act_sends.append(group)
        pltpu.make_async_remote_copy(
            src_ref=source,
            dst_ref=target,
            send_sem=send_sem.at[group],
            recv_sem=sem,
            device_id=device,
            device_id_type=MESH,
        ).start()

    def arrived(target, sem):
        pltpu.make_async_copy(target, target, sem).wait()

    pl.semaphore_wait(barrier, peers)

    for i in range(HALF_CHUNKS):
        block = gathered.at[m * HALF_CHUNKS + i, own]
        for dx in x_turns:
            send(block, block, half_sem.at[i, own], at(z, turn(x, dx, expert_ways), m))
        for dz in reversed(z_turns):
            send(block, block, half_sem.at[i, own], at(turn(z, dz, data_ways), x, m))

    row_at = lax.broadcasted_iota(jnp.int32, (PAD, LANES), 0)
    lane_at = lax.broadcasted_iota(jnp.int32, (PAD, LANES), 1)
    table = jnp.zeros((PAD, LANES), jnp.float32)
    for copy in id_copies:
        copy.wait()
    for r in range(tok):
        place = example_slots[example_ids[r]]
        expert = expert_ids[0, r]
        spread = LANES // 2 + place // order * PAD + place % order
        hit = (
            (lane_at == place) | (lane_at == example_count + expert) | (lane_at == spread)
        ) & (row_at == r)
        table = jnp.where(hit, 1.0, table)
    table = table.astype(jnp.bfloat16)
    grad_copy.wait()
    for q in range(data_ways):
        grad_send[q, :, :quarter] = padded(grad_v[:, q * quarter : (q + 1) * quarter])
        grad_send[q, :, quarter:] = table
    grad_got[own] = grad_send[z]
    for i in range(HALF_CHUNKS):
        c = m * HALF_CHUNKS + i
        for dz in z_turns:
            b = turn(z, dz, data_ways) * expert_ways + x
            block = gathered.at[c, b]
            arrived(block, half_sem.at[i, b])
            for dx in x_turns:
                send(block, block, half_sem.at[i, b], at(z, turn(x, dx, expert_ways), m))
            send(block, block, other_sem.at[i], at(z, x, other))
        for dz in [0] + z_turns:
            for dx in range(expert_ways):
                if dz or dx:
                    zz = turn(z, dz, data_ways)
                    send(
                        grad_send.at[zz],
                        grad_got.at[own],
                        grad_sem.at[0],
                        at(zz, turn(x, dx, expert_ways), m),
                        group=GRAD,
                    )
        for dz in [0] + z_turns:
            for dx in x_turns:
                b = turn(z, dz, data_ways) * expert_ways + turn(x, dx, expert_ways)
                block = gathered.at[c, b]
                arrived(block, half_sem.at[i, b])
                send(block, block, other_sem.at[i], at(z, x, other))

    def add_product(c, first):
        left = jnp.concatenate(
            [gathered[c, b].astype(jnp.float32) for b in range(blocks)], axis=0
        ).astype(jnp.bfloat16)
        span = pl.ds(pl.multiple_of(c * chunk, chunk), chunk)
        product = jnp.dot(left, basis[span, :], preferred_element_type=jnp.float32)
        total[...] = product if first else product + total[...]

    def gram(value):
        return lax.dot_general(
            value, value, (((1,), (1,)), ((), ())), preferred_element_type=jnp.float32
        )

    for i in range(HALF_CHUNKS):
        basis_copies[i].wait()
        add_product(chunk_order[i], i == 0)
    arrived(grad_got.at[pl.ds(0, blocks - 1)], grad_sem.at[0])
    out_copy.wait()
    grads = jnp.concatenate(
        [grad_got[b, :, :quarter].astype(jnp.float32) for b in range(blocks)], axis=0
    )
    scaled = (grads * lax.rsqrt(out_eigen[...] + eigen_floor)).astype(jnp.bfloat16)
    gram_out = gram(scaled) / FF
    mine = z * 2 + m
    tables = jnp.concatenate(
        [grad_got[b, :, quarter:].astype(jnp.float32) for b in range(blocks)], axis=0
    )

    def members(value):
        lanes = lax.broadcasted_iota(jnp.int32, value.shape, 1)
        chosen = jnp.where(lanes == example_count + x, value, 0.0)
        return value * jnp.sum(chosen, axis=1, keepdims=True)

    every_member = members(tables).astype(jnp.bfloat16)
    own_member = members(
        jnp.concatenate(
            [grad_got[z * 2 + i, :, quarter:].astype(jnp.float32) for i in range(2)], axis=0
        )
    )
    own_member = jnp.concatenate([own_member] * 3, axis=0).astype(jnp.bfloat16)

    def terms(value):
        high = value.astype(jnp.bfloat16).astype(jnp.float32)
        middle = (value - high).astype(jnp.bfloat16).astype(jnp.float32)
        return jnp.concatenate([high, middle, value - high - middle], axis=0).astype(jnp.bfloat16)

    for i in range(HALF_CHUNKS):
        c = chunk_order[HALF_CHUNKS + i]
        arrived(gathered.at[c, pl.ds(0, blocks - 1)], other_sem.at[i])
        basis_copies[HALF_CHUNKS + i].wait()
        add_product(c, False)

    in_copy.wait()
    rotated = (total[...] * lax.rsqrt(in_eigen[...] + eigen_floor)).astype(jnp.bfloat16)
    gram_in = gram(rotated) / D

    part_send[...] = jnp.concatenate([gram_in, gram_out], axis=1).reshape(
        data_ways, 2 * PAD, LANES
    )
    for dz in [0] + z_turns:
        for dm in range(2):
            if dz or dm:
                zz, mm = turn(z, dz, data_ways), turn(m, dm, 2)
                send(
                    part_send.at[zz],
                    part_got.at[mine],
                    part_sem.at[0],
                    at(zz, x, mm),
                    group=PART,
                )
    part_got[mine] = part_send[z]
    arrived(part_got.at[pl.ds(0, blocks - 1)], part_sem.at[0])
    sums = jnp.sum(part_got[...], axis=0)
    weights = sums[:, :rows] * sums[:, rows:]
    right = jnp.dot(terms(weights), every_member, preferred_element_type=jnp.float32)
    right = right[: 2 * PAD] + right[2 * PAD : 4 * PAD] + right[4 * PAD :]
    pairs = lax.dot_general(
        own_member,
        terms(right),
        (((0,), (0,)), ((), ())),
        preferred_element_type=jnp.float32,
    )
    kernel_send[...] = pairs[LANES // 2 :].reshape(blocks, PAD, LANES)
    for dz in [0] + z_turns:
        for dx in range(expert_ways):
            if dz or dx:
                zz, xx = turn(z, dz, data_ways), turn(x, dx, expert_ways)
                send(
                    kernel_send.at[zz * expert_ways + xx],
                    kernel_got.at[own],
                    kernel_sem.at[0],
                    at(zz, xx, m),
                    group=KERNEL,
                )
    kernel_got[own] = kernel_send[own]
    arrived(kernel_got.at[pl.ds(0, blocks - 1)], kernel_sem.at[0])
    system = jnp.sum(kernel_got[...], axis=0)

    work = system
    for k in range(order):
        column = jnp.sum(jnp.where(lane_at == own * order + k, system, 0.0), axis=1, keepdims=True)
        column = column + jnp.where(row_at == k, ridge_term, 0.0)
        work = jnp.where(lane_at == LANES // 2 + k, column, work)
    for k in range(order):
        column = jnp.sum(jnp.where(lane_at == LANES // 2 + k, work, 0.0), axis=1, keepdims=True)
        pivot_row = work[k : k + 1, :] / column[k : k + 1, :]
        work = jnp.where(row_at == k, pivot_row, work - column * pivot_row)
    out_ref[...] = work[:order, :example_count]
    for group in range(ACT_GROUPS):
        arrived(gathered.at[0, pl.ds(0, blocks - 1)], send_sem.at[group])
    arrived(grad_got.at[pl.ds(0, blocks - 1)], send_sem.at[GRAD])
    arrived(part_got.at[pl.ds(0, blocks - 1)], send_sem.at[PART])
    arrived(kernel_got.at[pl.ds(0, blocks - 1)], send_sem.at[KERNEL])


def fused(
    activations,
    gradients,
    expert_ids,
    example_ids,
    example_slots,
    eigenbasis,
    input_eigen,
    output_eigen,
):
    data_ways = lax.axis_size("dp")
    expert_ways = lax.axis_size("expert")
    tok = activations.shape[0]
    example_count = example_slots.shape[0]
    blocks = data_ways * expert_ways
    depth, width = eigenbasis.shape[1:]
    chunks = 2 * HALF_CHUNKS
    chunk = depth // chunks
    quarter = gradients.shape[1] // data_ways
    dma = pltpu.SemaphoreType.DMA
    far = pl.BlockSpec(memory_space=pltpu.HBM)
    return pl.pallas_call(
        functools.partial(fused_kernel, (data_ways, expert_ways, tok, example_count)),
        out_shape=jax.ShapeDtypeStruct((example_count // blocks, example_count), jnp.float32),
        in_specs=[far] * 8,
        out_specs=pl.BlockSpec(memory_space=pltpu.VMEM),
        scratch_shapes=[
            pltpu.SMEM((1, tok), jnp.int32),
            pltpu.SMEM((tok,), jnp.int32),
            pltpu.SMEM((example_count,), jnp.int32),
            pltpu.VMEM(activations.shape, jnp.bfloat16),
            pltpu.VMEM(gradients.shape, jnp.bfloat16),
            pltpu.VMEM(input_eigen.shape, jnp.float32),
            pltpu.VMEM((1, quarter), jnp.float32),
            pltpu.VMEM((depth, width), jnp.bfloat16),
            pltpu.VMEM((chunks, blocks, PAD, chunk), jnp.bfloat16),
            pltpu.VMEM((data_ways, PAD, quarter + LANES), jnp.bfloat16),
            pltpu.VMEM((blocks, PAD, quarter + LANES), jnp.bfloat16),
            pltpu.VMEM((data_ways, 2 * PAD, LANES), jnp.float32),
            pltpu.VMEM((blocks, 2 * PAD, LANES), jnp.float32),
            pltpu.VMEM((blocks, PAD, LANES), jnp.float32),
            pltpu.VMEM((blocks, PAD, LANES), jnp.float32),
            pltpu.VMEM((blocks * PAD, width), jnp.float32),
            dma((7,)),
            dma((chunks,)),
            dma((KERNEL + 1,)),
            dma((HALF_CHUNKS, blocks)),
            dma((HALF_CHUNKS,)),
            dma((1,)),
            dma((1,)),
            dma((1,)),
        ],
        compiler_params=pltpu.CompilerParams(
            collective_id=0, has_side_effects=True, vmem_limit_bytes=60 * 1024 * 1024
        ),
    )(
        activations,
        gradients,
        expert_ids.T,
        example_ids,
        example_slots,
        eigenbasis,
        input_eigen,
        output_eigen,
    )


def fits_fused(mesh, tok, example_count):
    data_ways, expert_ways = mesh.shape["dp"], mesh.shape["expert"]
    blocks = data_ways * expert_ways
    order = example_count // blocks
    return (
        mesh.shape["mp"] == 2
        and data_ways * 2 == blocks
        and blocks * PAD * 2 == LANES
        and tok <= PAD
        and order <= PAD
        and example_count + expert_ways <= LANES // 2
    )


def on_any_slice(mesh, activations, gradients, expert_ids, example_ids, example_slots, *factors):
    use = fits_fused(mesh, activations.shape[0], example_slots.shape[0])
    return (fused if use else on_device)(
        activations, gradients, expert_ids, example_ids, example_slots, *factors
    )


def solution(mesh):
    placed = (
        P(("groups", "dp", "expert"), None),
        P(("groups", "dp", "expert"), "mp"),
        P(("groups", "dp", "expert"), None),
        P(("groups", "dp", "expert")),
        P("groups"),
        P("expert", None, ("dp", "mp")),
        P("expert", ("dp", "mp")),
        P("expert", "mp"),
    )
    return jax.shard_map(
        functools.partial(on_any_slice, mesh),
        mesh=mesh,
        in_specs=placed,
        out_specs=P(("groups", "dp", "expert"), None),
        check_vma=False,
    )
```

```python
import functools

import jax
import jax.numpy as jnp
from jax import lax
from jax.experimental import pallas as pl
from jax.experimental.pallas import tpu as pltpu
from jax.sharding import PartitionSpec as P

D = 6144
FF = 8192
CAP = 5


eigen_floor = 0.01
ridge_term = 500.0


def shifted(x, axis, by):
    size = lax.axis_size(axis)
    return lax.ppermute(x, axis, [(i, (i + by) % size) for i in range(size)])


def member_table(slot_list, example_count):
    return (slot_list[:, None] == jnp.arange(example_count, dtype=jnp.int32)[None, :]).astype(
        jnp.float32
    )


def solve_system(system_rows, first_row):
    order = system_rows.shape[0]
    square = lax.dynamic_slice_in_dim(system_rows, first_row, order, 1)
    square = square + ridge_term * jnp.eye(order, dtype=system_rows.dtype)
    factor = jnp.linalg.cholesky(square)
    middle = lax.linalg.triangular_solve(factor, system_rows, left_side=True, lower=True)
    return lax.linalg.triangular_solve(factor, middle, left_side=True, lower=True, transpose_a=True)


def on_device(
    activations,
    gradients,
    expert_ids,
    example_ids,
    example_slots,
    eigenbasis,
    input_eigen,
    output_eigen,
):
    data_ways = lax.axis_size("dp")
    expert_ways = lax.axis_size("expert")
    example_count = example_slots.shape[0]
    slot_width = expert_ways * CAP
    chosen = expert_ids[:, 0]
    onehot = (chosen[:, None] == jnp.arange(expert_ways, dtype=jnp.int32)[None, :]).astype(
        jnp.int32
    )
    position = jnp.sum((jnp.cumsum(onehot, axis=0) - onehot) * onehot, axis=1)
    target = chosen * CAP + position
    placing = target[None, :] == jnp.arange(slot_width, dtype=jnp.int32)[:, None]
    placing_table = placing.astype(jnp.bfloat16)
    lookup = (example_ids[:, None] == jnp.arange(example_count, dtype=jnp.int32)[None, :]).astype(
        jnp.int32
    )
    row_slot = jnp.sum(lookup * example_slots[None, :], axis=1)
    send_inputs = jnp.dot(placing_table, activations, preferred_element_type=jnp.float32).astype(
        jnp.bfloat16
    )
    send_grads = jnp.dot(placing_table, gradients, preferred_element_type=jnp.float32).astype(
        jnp.bfloat16
    )
    send_slots = jnp.sum(jnp.where(placing, row_slot[None, :] + 1, 0), axis=1) - 1
    got_inputs, got_grads, got_slots = (
        lax.all_to_all(
            send_inputs.reshape(expert_ways, CAP, -1),
            "expert",
            split_axis=0,
            concat_axis=0,
            tiled=True,
        ),
        lax.all_to_all(
            send_grads.reshape(expert_ways, CAP, -1),
            "expert",
            split_axis=0,
            concat_axis=0,
            tiled=True,
        ),
        lax.all_to_all(
            send_slots.reshape(expert_ways, CAP), "expert", split_axis=0, concat_axis=0, tiled=True
        ),
    )
    own_inputs = got_inputs.reshape(slot_width, -1)
    own_grads = got_grads.reshape(slot_width, -1)
    own_slots = got_slots.reshape(slot_width)
    basis_block = eigenbasis[0]
    scale_in = lax.rsqrt(input_eigen[0] + eigen_floor)
    rotated = (
        jnp.dot(
            lax.all_gather(own_inputs, "dp", axis=0, tiled=True),
            basis_block,
            preferred_element_type=jnp.float32,
        )
        * scale_in
    ).astype(jnp.bfloat16)
    gram_part = (
        lax.dot_general(
            rotated, rotated, (((1,), (1,)), ((), ())), preferred_element_type=jnp.float32
        )
        / D
    )
    dp_index = lax.axis_index("dp")
    gram_in = lax.psum(gram_part, ("dp", "mp"))
    own_gram = lax.dynamic_slice_in_dim(gram_in, dp_index * slot_width, slot_width, 0)
    scaled = (own_grads.astype(jnp.float32) * lax.rsqrt(output_eigen[0] + eigen_floor)).astype(
        jnp.bfloat16
    )
    own_members = member_table(own_slots, example_count)

    def pair_terms(peer_grads, peer_slots, first_row):
        gram_out = (
            lax.dot_general(
                scaled, peer_grads, (((1,), (1,)), ((), ())), preferred_element_type=jnp.float32
            )
            / FF
        )
        weights = lax.dynamic_slice_in_dim(own_gram, first_row, peer_grads.shape[0], 1) * gram_out
        return jnp.dot(
            weights, member_table(peer_slots, example_count), precision=lax.Precision.HIGHEST
        )

    one_way = pair_terms(scaled, own_slots, dp_index * slot_width)
    both_ways = jnp.zeros_like(one_way)
    for offset in range(1, data_ways // 2 + 1):
        peer_grads, peer_slots = shifted((scaled, own_slots), "dp", offset)
        source_index = (dp_index - offset) % data_ways
        contribution = pair_terms(peer_grads, peer_slots, source_index * slot_width)
        if 2 * offset < data_ways:
            both_ways = both_ways + contribution
        else:
            one_way = one_way + contribution
    kernel = lax.dot_general(
        own_members, one_way + both_ways, (((0,), (0,)), ((), ())), precision=lax.Precision.HIGHEST
    )
    mirrored = lax.dot_general(
        own_members, both_ways, (((0,), (0,)), ((), ())), precision=lax.Precision.HIGHEST
    )
    kernel = kernel + mirrored.T
    shares = lax.psum_scatter(kernel, ("dp", "expert", "mp"), scatter_dimension=0, tiled=True)
    system_rows = lax.all_gather(shares, "mp", axis=0, tiled=True)
    first_row = (dp_index * expert_ways + lax.axis_index("expert")) * system_rows.shape[0]
    return solve_system(system_rows, first_row)


MESH = pl.DeviceIdType.MESH
PAD = 8
LANES = 128
HALF_CHUNKS = 1
ACT_GROUPS = 2 * HALF_CHUNKS
GRAD, PART, KERNEL = ACT_GROUPS, ACT_GROUPS + 1, ACT_GROUPS + 2


def fused_kernel(
    sizes,
    act_hbm,
    grad_hbm,
    expert_ids_hbm,
    example_ids_hbm,
    example_slots_hbm,
    basis_hbm,
    in_eigen_hbm,
    out_eigen_hbm,
    out_ref,
    expert_ids,
    example_ids,
    example_slots,
    act_v,
    grad_v,
    in_eigen,
    out_eigen,
    basis,
    gathered,
    grad_send,
    grad_got,
    part_send,
    part_got,
    kernel_send,
    kernel_got,
    total,
    local_sem,
    basis_sem,
    send_sem,
    half_sem,
    other_sem,
    grad_sem,
    part_sem,
    kernel_sem,
):
    data_ways, expert_ways, tok, example_count = sizes
    blocks = data_ways * expert_ways
    order = example_count // blocks
    rows = blocks * PAD
    z, x, m = lax.axis_index("dp"), lax.axis_index("expert"), lax.axis_index("mp")
    own = z * expert_ways + x
    chunk = gathered.shape[3]
    quarter = out_eigen.shape[1]
    chunks = gathered.shape[0]

    def at(zz, xx, mm):
        return {"dp": zz, "expert": xx, "mp": mm}

    def turn(i, by, size):
        return lax.rem(i + by, size)

    z_turns = sorted(range(1, data_ways), key=lambda d: (min(d, data_ways - d), d))
    x_turns = range(1, expert_ways)
    other = 1 - m

    barrier = pltpu.get_barrier_semaphore()
    peers = 0
    for dz in range(data_ways):
        for dx in range(expert_ways):
            for dm in range(2):
                if (dz or dx or dm) and not (dx and dm):
                    pl.semaphore_signal(
                        barrier,
                        inc=1,
                        device_id=at(
                            turn(z, dz, data_ways), turn(x, dx, expert_ways), turn(m, dm, 2)
                        ),
                        device_id_type=MESH,
                    )
                    peers += 1

    act_copy = pltpu.make_async_copy(act_hbm, act_v, local_sem.at[0])
    act_copy.start()
    id_copies = [
        pltpu.make_async_copy(source, target, local_sem.at[4 + i])
        for i, (source, target) in enumerate(
            (
                (expert_ids_hbm, expert_ids),
                (example_ids_hbm, example_ids),
                (example_slots_hbm, example_slots),
            )
        )
    ]
    for copy in id_copies:
        copy.start()
    grad_copy = pltpu.make_async_copy(grad_hbm, grad_v, local_sem.at[1])
    grad_copy.start()
    chunk_order = [
        m * HALF_CHUNKS + i for i in range(HALF_CHUNKS)
    ] + [other * HALF_CHUNKS + i for i in range(HALF_CHUNKS)]
    basis_copies = []
    for i, c in enumerate(chunk_order):
        span = pl.ds(pl.multiple_of(c * chunk, chunk), chunk)
        copy = pltpu.make_async_copy(
            basis_hbm.at[0, span, :], basis.at[span, :], basis_sem.at[i]
        )
        copy.start()
        basis_copies.append(copy)
    in_copy = pltpu.make_async_copy(in_eigen_hbm, in_eigen, local_sem.at[2])
    in_copy.start()
    out_copy = pltpu.make_async_copy(
        out_eigen_hbm.at[:, pl.ds(pl.multiple_of(z * quarter, quarter), quarter)],
        out_eigen,
        local_sem.at[3],
    )
    out_copy.start()

    def padded(value):
        value = value.astype(jnp.float32)
        fill = jnp.zeros((PAD - tok, value.shape[1]), jnp.float32)
        return jnp.concatenate([value, fill], axis=0).astype(jnp.bfloat16)

    act_copy.wait()
    for c in range(chunks):
        gathered[c, own] = padded(act_v[:, c * chunk : (c + 1) * chunk])

    act_sends = []

    def send(source, target, sem, device, group=None):
        if group is None:
            group = len(act_sends) // (blocks - 1)
            act_sends.append(group)
        pltpu.make_async_remote_copy(
            src_ref=source,
            dst_ref=target,
            send_sem=send_sem.at[group],
            recv_sem=sem,
            device_id=device,
            device_id_type=MESH,
        ).start()

    def arrived(target, sem):
        pltpu.make_async_copy(target, target, sem).wait()

    row_at = lax.broadcasted_iota(jnp.int32, (PAD, LANES), 0)
    lane_at = lax.broadcasted_iota(jnp.int32, (PAD, LANES), 1)
    table = jnp.zeros((PAD, LANES), jnp.float32)
    for copy in id_copies:
        copy.wait()
    for r in range(tok):
        place = example_slots[example_ids[r]]
        expert = expert_ids[0, r]
        spread = LANES // 2 + place // order * PAD + place % order
        hit = (
            (lane_at == place) | (lane_at == example_count + expert) | (lane_at == spread)
        ) & (row_at == r)
        table = jnp.where(hit, 1.0, table)
    table = table.astype(jnp.bfloat16)
    grad_copy.wait()
    for q in range(data_ways):
        grad_send[q, :, :quarter] = padded(grad_v[:, q * quarter : (q + 1) * quarter])
        grad_send[q, :, quarter:] = table
    grad_got[own] = grad_send[z]

    pl.semaphore_wait(barrier, peers)

    for i in range(HALF_CHUNKS):
        block = gathered.at[m * HALF_CHUNKS + i, own]
        for dx in x_turns:
            send(block, block, half_sem.at[i, own], at(z, turn(x, dx, expert_ways), m))
        for dz in z_turns:
            send(block, block, half_sem.at[i, own], at(turn(z, dz, data_ways), x, m))

    for i in range(HALF_CHUNKS):
        c = m * HALF_CHUNKS + i
        for dz in z_turns:
            b = turn(z, dz, data_ways) * expert_ways + x
            block = gathered.at[c, b]
            arrived(block, half_sem.at[i, b])
            for dx in x_turns:
                send(block, block, half_sem.at[i, b], at(z, turn(x, dx, expert_ways), m))
            send(block, block, other_sem.at[i], at(z, x, other))
        for dz in [0] + z_turns:
            for dx in range(expert_ways):
                if dz or dx:
                    zz = turn(z, dz, data_ways)
                    send(
                        grad_send.at[zz],
                        grad_got.at[own],
                        grad_sem.at[0],
                        at(zz, turn(x, dx, expert_ways), m),
                        group=GRAD,
                    )
        for dz in [0] + z_turns:
            for dx in x_turns:
                b = turn(z, dz, data_ways) * expert_ways + turn(x, dx, expert_ways)
                block = gathered.at[c, b]
                arrived(block, half_sem.at[i, b])
                send(block, block, other_sem.at[i], at(z, x, other))

    def add_product(c, first):
        left = jnp.concatenate(
            [gathered[c, b].astype(jnp.float32) for b in range(blocks)], axis=0
        ).astype(jnp.bfloat16)
        span = pl.ds(pl.multiple_of(c * chunk, chunk), chunk)
        product = jnp.dot(left, basis[span, :], preferred_element_type=jnp.float32)
        total[...] = product if first else product + total[...]

    def gram(value):
        return lax.dot_general(
            value, value, (((1,), (1,)), ((), ())), preferred_element_type=jnp.float32
        )

    for i in range(HALF_CHUNKS):
        basis_copies[i].wait()
        add_product(chunk_order[i], i == 0)
    arrived(grad_got.at[pl.ds(0, blocks - 1)], grad_sem.at[0])
    out_copy.wait()
    grads = jnp.concatenate(
        [grad_got[b, :, :quarter].astype(jnp.float32) for b in range(blocks)], axis=0
    )
    scaled = (grads * lax.rsqrt(out_eigen[...] + eigen_floor)).astype(jnp.bfloat16)
    gram_out = gram(scaled) / FF
    mine = z * 2 + m
    tables = jnp.concatenate(
        [grad_got[b, :, quarter:].astype(jnp.float32) for b in range(blocks)], axis=0
    )

    def members(value):
        lanes = lax.broadcasted_iota(jnp.int32, value.shape, 1)
        chosen = jnp.where(lanes == example_count + x, value, 0.0)
        return value * jnp.sum(chosen, axis=1, keepdims=True)

    every_member = members(tables).astype(jnp.bfloat16)
    own_member = members(
        jnp.concatenate(
            [grad_got[z * 2 + i, :, quarter:].astype(jnp.float32) for i in range(2)], axis=0
        )
    )
    own_member = jnp.concatenate([own_member] * 3, axis=0).astype(jnp.bfloat16)

    def terms(value):
        high = value.astype(jnp.bfloat16).astype(jnp.float32)
        middle = (value - high).astype(jnp.bfloat16).astype(jnp.float32)
        return jnp.concatenate([high, middle, value - high - middle], axis=0).astype(jnp.bfloat16)

    for i in range(HALF_CHUNKS):
        c = chunk_order[HALF_CHUNKS + i]
        arrived(gathered.at[c, pl.ds(0, blocks - 1)], other_sem.at[i])
        basis_copies[HALF_CHUNKS + i].wait()
        add_product(c, False)

    in_copy.wait()
    rotated = (total[...] * lax.rsqrt(in_eigen[...] + eigen_floor)).astype(jnp.bfloat16)
    gram_in = gram(rotated) / D

    part_send[...] = jnp.concatenate([gram_in, gram_out], axis=1).reshape(
        data_ways, 2 * PAD, LANES
    )
    for dz in [0] + z_turns:
        for dm in range(2):
            if dz or dm:
                zz, mm = turn(z, dz, data_ways), turn(m, dm, 2)
                send(
                    part_send.at[zz],
                    part_got.at[mine],
                    part_sem.at[0],
                    at(zz, x, mm),
                    group=PART,
                )
    part_got[mine] = part_send[z]
    arrived(part_got.at[pl.ds(0, blocks - 1)], part_sem.at[0])
    sums = jnp.sum(part_got[...], axis=0)
    weights = sums[:, :rows] * sums[:, rows:]
    right = jnp.dot(terms(weights), every_member, preferred_element_type=jnp.float32)
    right = right[: 2 * PAD] + right[2 * PAD : 4 * PAD] + right[4 * PAD :]
    pairs = lax.dot_general(
        own_member,
        terms(right),
        (((0,), (0,)), ((), ())),
        preferred_element_type=jnp.float32,
    )
    kernel_send[...] = pairs[LANES // 2 :].reshape(blocks, PAD, LANES)
    for dz in [0] + z_turns:
        for dx in range(expert_ways):
            if dz or dx:
                zz, xx = turn(z, dz, data_ways), turn(x, dx, expert_ways)
                send(
                    kernel_send.at[zz * expert_ways + xx],
                    kernel_got.at[own],
                    kernel_sem.at[0],
                    at(zz, xx, m),
                    group=KERNEL,
                )
    kernel_got[own] = kernel_send[own]
    arrived(kernel_got.at[pl.ds(0, blocks - 1)], kernel_sem.at[0])
    system = jnp.sum(kernel_got[...], axis=0)

    work = system
    for k in range(order):
        column = jnp.sum(jnp.where(lane_at == own * order + k, system, 0.0), axis=1, keepdims=True)
        column = column + jnp.where(row_at == k, ridge_term, 0.0)
        work = jnp.where(lane_at == LANES // 2 + k, column, work)
    for k in range(order):
        column = jnp.sum(jnp.where(lane_at == LANES // 2 + k, work, 0.0), axis=1, keepdims=True)
        pivot_row = work[k : k + 1, :] / column[k : k + 1, :]
        work = jnp.where(row_at == k, pivot_row, work - column * pivot_row)
    out_ref[...] = work[:order, :example_count]
    for group in range(ACT_GROUPS):
        arrived(gathered.at[0, pl.ds(0, blocks - 1)], send_sem.at[group])
    arrived(grad_got.at[pl.ds(0, blocks - 1)], send_sem.at[GRAD])
    arrived(part_got.at[pl.ds(0, blocks - 1)], send_sem.at[PART])
    arrived(kernel_got.at[pl.ds(0, blocks - 1)], send_sem.at[KERNEL])


def fused(
    activations,
    gradients,
    expert_ids,
    example_ids,
    example_slots,
    eigenbasis,
    input_eigen,
    output_eigen,
):
    data_ways = lax.axis_size("dp")
    expert_ways = lax.axis_size("expert")
    tok = activations.shape[0]
    example_count = example_slots.shape[0]
    blocks = data_ways * expert_ways
    depth, width = eigenbasis.shape[1:]
    chunks = 2 * HALF_CHUNKS
    chunk = depth // chunks
    quarter = gradients.shape[1] // data_ways
    dma = pltpu.SemaphoreType.DMA
    far = pl.BlockSpec(memory_space=pltpu.HBM)
    return pl.pallas_call(
        functools.partial(fused_kernel, (data_ways, expert_ways, tok, example_count)),
        out_shape=jax.ShapeDtypeStruct((example_count // blocks, example_count), jnp.float32),
        in_specs=[far] * 8,
        out_specs=pl.BlockSpec(memory_space=pltpu.VMEM),
        scratch_shapes=[
            pltpu.SMEM((1, tok), jnp.int32),
            pltpu.SMEM((tok,), jnp.int32),
            pltpu.SMEM((example_count,), jnp.int32),
            pltpu.VMEM(activations.shape, jnp.bfloat16),
            pltpu.VMEM(gradients.shape, jnp.bfloat16),
            pltpu.VMEM(input_eigen.shape, jnp.float32),
            pltpu.VMEM((1, quarter), jnp.float32),
            pltpu.VMEM((depth, width), jnp.bfloat16),
            pltpu.VMEM((chunks, blocks, PAD, chunk), jnp.bfloat16),
            pltpu.VMEM((data_ways, PAD, quarter + LANES), jnp.bfloat16),
            pltpu.VMEM((blocks, PAD, quarter + LANES), jnp.bfloat16),
            pltpu.VMEM((data_ways, 2 * PAD, LANES), jnp.float32),
            pltpu.VMEM((blocks, 2 * PAD, LANES), jnp.float32),
            pltpu.VMEM((blocks, PAD, LANES), jnp.float32),
            pltpu.VMEM((blocks, PAD, LANES), jnp.float32),
            pltpu.VMEM((blocks * PAD, width), jnp.float32),
            dma((7,)),
            dma((chunks,)),
            dma((KERNEL + 1,)),
            dma((HALF_CHUNKS, blocks)),
            dma((HALF_CHUNKS,)),
            dma((1,)),
            dma((1,)),
            dma((1,)),
        ],
        compiler_params=pltpu.CompilerParams(
            collective_id=0, has_side_effects=True, vmem_limit_bytes=60 * 1024 * 1024
        ),
    )(
        activations,
        gradients,
        expert_ids.T,
        example_ids,
        example_slots,
        eigenbasis,
        input_eigen,
        output_eigen,
    )


def fits_fused(mesh, tok, example_count):
    data_ways, expert_ways = mesh.shape["dp"], mesh.shape["expert"]
    blocks = data_ways * expert_ways
    order = example_count // blocks
    return (
        mesh.shape["mp"] == 2
        and data_ways * 2 == blocks
        and blocks * PAD * 2 == LANES
        and tok <= PAD
        and order <= PAD
        and example_count + expert_ways <= LANES // 2
    )


def on_any_slice(mesh, activations, gradients, expert_ids, example_ids, example_slots, *factors):
    use = fits_fused(mesh, activations.shape[0], example_slots.shape[0])
    return (fused if use else on_device)(
        activations, gradients, expert_ids, example_ids, example_slots, *factors
    )


def solution(mesh):
    placed = (
        P(("groups", "dp", "expert"), None),
        P(("groups", "dp", "expert"), "mp"),
        P(("groups", "dp", "expert"), None),
        P(("groups", "dp", "expert")),
        P("groups"),
        P("expert", None, ("dp", "mp")),
        P("expert", ("dp", "mp")),
        P("expert", "mp"),
    )
    return jax.shard_map(
        functools.partial(on_any_slice, mesh),
        mesh=mesh,
        in_specs=placed,
        out_specs=P(("groups", "dp", "expert"), None),
        check_vma=False,
    )
```
